512 devices in a mesh: deg: 64 (over y, z_lo, core), row: 8 (over x, z_hi).
Axes of the slice: x: 4, y: 8, z: 8 (z_hi: 2, z_lo: 4; z = z_hi * 4 + z_lo), core: 2. Of those that a mesh axis runs over, the one named last changes fastest.
Arguments:
- left_factor: float32 [16384, 16, 64], P('deg', 'row'), may hold values from 0 to 7340032, as said below
- right_factor: float32 [16384, 64, 64], P('deg', 'row'), may hold values from 0 to 7340032, as said below
Outputs:
- product_coeffs: float32 [32768, 16, 64], P('deg', 'row')
The draws below stay inside these ranges and needn't reach their ends.
Inputs may be any that keep to these rules, and one draw needn't show every extreme that they name: `left_factor`: whole numbers, each a residue modulo the prime 7340033; both ends occur. `right_factor`: whole numbers, each a residue modulo the prime 7340033; both ends occur.
All inputs are finite; a program needn't handle non-finite values.
Results may differ from the reference program's by a relative error of at most 0.0003.
Values sent between devices are 32-bit elements; how exact they have to be, the bound alone decides.
A program may use at most 128 MiB of HBM per device.

```python
import math
import jax
import jax.numpy as jnp
from jax import lax

DEG_IN = 16384
INNER = 256
KD = 64
CD = 64
ROWS = 16


def residues(key, shape):
    values = jax.random.randint(key, shape, 0, 7340033).astype(jnp.float32)
    values = values.at[0, 0, 0].set(7340032.0)
    return values.at[0, 0, 1].set(0.0)


def draw_left_factor(key, part):
    key = jax.random.fold_in(key, 11)
    return residues(key, (DEG_IN, ROWS, KD))


def draw_right_factor(key, part):
    key = jax.random.fold_in(key, 12)
    return residues(key, (DEG_IN, KD, CD))


def setup_inputs(seed: int = 0) -> dict:
    key_of = jax.random.split(jax.random.key(seed), 3)
    left_factor = draw_left_factor(jax.random.fold_in(key_of[2], 71), 0)
    right_factor = draw_right_factor(jax.random.fold_in(key_of[2], 71), 0)
    return {"left_factor": left_factor, "right_factor": right_factor}


modulus = 7340033
generator = 3


def mulmod(values, factor):
    high = factor // 65536
    middle = (factor // 256) % 256
    lowest = factor % 256
    result = (values * high) % modulus
    result = (result * 256) % modulus
    result = (result + (values * middle) % modulus) % modulus
    result = (result * 256) % modulus
    return (result + (values * lowest) % modulus) % modulus


def power_table(exponents, length):
    factor = pow(generator, (modulus - 1) // length, modulus)
    result = jnp.ones_like(exponents)
    position = 1
    while position < length:
        chosen = (exponents // position) % 2 == 1
        result = jnp.where(chosen, mulmod(result, factor), result)
        factor = factor * factor % modulus
        position = position * 2
    return result


def negated(exponents, length):
    return (length - exponents % length) % length


def split_limbs(values):
    integers = values.astype(jnp.int32)
    return [(integers % 256).astype(jnp.float32), ((integers // 256) % 256).astype(jnp.float32), (integers // 65536).astype(jnp.float32)]


def mod_contract(pattern, left_values, right_values):
    left_limbs = split_limbs(left_values)
    right_limbs = split_limbs(right_values)
    shifts = [1, 256, 65536]
    accumulated = None
    for left_limb in range(3):
        partial_value = None
        for right_limb in range(3):
            product = jnp.einsum(pattern, left_limbs[left_limb], right_limbs[right_limb], precision=lax.Precision.HIGHEST)
            contribution = mulmod(product.astype(jnp.int32) % modulus, shifts[right_limb])
            partial_value = contribution if partial_value is None else (partial_value + contribution) % modulus
        contribution = mulmod(partial_value, shifts[left_limb])
        accumulated = contribution if accumulated is None else (accumulated + contribution) % modulus
    return accumulated.astype(jnp.float32)


def reference(left_factor, right_factor):
    length = 2 * DEG_IN
    first_count = DEG_IN // INNER
    frequencies = 2 * first_count
    low_index = jnp.arange(first_count, dtype=jnp.int32)
    freq_index = jnp.arange(frequencies, dtype=jnp.int32)
    inner_index = jnp.arange(INNER, dtype=jnp.int32)
    table_one = power_table((INNER * low_index[:, None] * freq_index[None, :]) % length, length)
    twiddle = power_table((freq_index[:, None] * inner_index[None, :]) % length, length)
    table_two = power_table((frequencies * inner_index[:, None] * inner_index[None, :]) % length, length)
    back_two = power_table(negated(frequencies * inner_index[:, None] * inner_index[None, :], length), length)
    back_twiddle = power_table(negated(freq_index[:, None] * inner_index[None, :], length), length)
    back_one = mulmod(power_table(negated(INNER * freq_index[:, None] * freq_index[None, :], length), length), pow(length, modulus - 2, modulus))

    def forward_block(values):
        sectioned = mod_contract("nsp,nk->ksp", values, table_one)
        sectioned = mulmod(sectioned.astype(jnp.int32), twiddle[:, :, None]).astype(jnp.float32)
        return mod_contract("ksp,sj->kjp", sectioned, table_two)

    def forward_all(values):
        width_all = values.shape[1]
        block_width = math.gcd(256, width_all)
        block_count = width_all // block_width
        shaped = values.reshape(first_count, INNER, block_count, block_width).transpose(2, 0, 1, 3)
        spectra = lax.map(forward_block, shaped)
        return spectra.transpose(1, 2, 0, 3).reshape(frequencies, INNER, width_all)

    left_spec = forward_all(left_factor.reshape(DEG_IN, ROWS * KD)).reshape(frequencies, INNER, ROWS, KD)
    right_spec = forward_all(right_factor.reshape(DEG_IN, KD * CD)).reshape(frequencies, INNER, KD, CD)

    def multiply(operands):
        return mod_contract("frk,fkc->frc", operands[0], operands[1])

    product_spec = lax.map(multiply, (left_spec, right_spec))

    def inverse_block(values):
        sectioned = mod_contract("kjp,jn->knp", values, back_two)
        sectioned = mulmod(sectioned.astype(jnp.int32), back_twiddle[:, :, None]).astype(jnp.float32)
        return mod_contract("knp,km->mnp", sectioned, back_one)

    width_out = ROWS * CD
    block_width = math.gcd(256, width_out)
    block_count = width_out // block_width
    shaped = product_spec.reshape(frequencies, INNER, block_count, block_width).transpose(2, 0, 1, 3)
    coeffs = lax.map(inverse_block, shaped).transpose(1, 2, 0, 3).reshape(length, ROWS, CD)
    return coeffs / modulus
```

```python
import numpy as np
import jax
import jax.numpy as jnp
from jax import lax
from jax.sharding import PartitionSpec as P

modulus = 7340033
generator = 3
inverse_modulus = 1.0 / modulus
modulus_high = float(modulus - 1)

BLOCK = 256
POINTS = 2 * BLOCK
KD = 64
CD = 64


def powers(root, exponents, order):
    table = np.ones(order, np.int64)
    for position in range(1, order):
        table[position] = table[position - 1] * root % modulus
    return table[exponents % order]


def digit_rows(values):
    centred = np.where(values > modulus // 2, values - modulus, values)
    digits = []
    for _ in range(2):
        low = (centred + 128) % 256 - 128
        digits.append(low)
        centred = (centred - low) // 256
    digits.append(centred)
    return np.concatenate(digits, axis=0).astype(jnp.bfloat16)


def stacked_table(values):
    return digit_rows(
        np.concatenate([values * 256**digit % modulus for digit in range(3)], axis=1)
    )


def point_table():
    root = pow(generator, (modulus - 1) // POINTS, modulus)
    exponents = np.arange(POINTS)[:, None] * np.arange(BLOCK)[None, :]
    return stacked_table(powers(root, exponents, POINTS))


def block_table(blocks):
    root = pow(generator, (modulus - 1) // (2 * blocks), modulus)
    exponents = np.arange(2 * blocks)[:, None] * np.arange(blocks)[None, :]
    return stacked_table(powers(root, exponents, 2 * blocks))


def block_back_table(blocks, sign):
    length = 2 * blocks
    root = pow(generator, (modulus - 1) // length, modulus)
    exponents = -np.arange(length)[:, None] * np.arange(length)[None, :]
    carry = 1 + sign * powers(root, np.arange(length), length)
    return stacked_table(powers(root, exponents, length) * carry[None, :] % modulus)


def point_back_table(blocks):
    root = pow(generator, (modulus - 1) // POINTS, modulus)
    exponents = -np.arange(BLOCK)[:, None] * np.arange(POINTS)[None, :]
    scale = pow(2 * blocks * POINTS, modulus - 2, modulus)
    return powers(root, exponents, POINTS) * scale % modulus


def reduced(values):
    quotient = jnp.round(values * inverse_modulus)
    return (values - quotient * modulus_high) - quotient


def folded(sums):
    low, middle, high = sums
    return reduced(reduced((reduced(high * 256.0) + middle) * 256.0) + low)


def digits_of(values):
    high = jnp.round(values * (1.0 / 65536.0))
    rest = values - high * 65536.0
    middle = jnp.round(rest * (1.0 / 256.0))
    low = rest - middle * 256.0
    return [low.astype(jnp.bfloat16), middle.astype(jnp.bfloat16), high.astype(jnp.bfloat16)]


def transformed(table, values):
    stacked = jnp.concatenate(digits_of(values), axis=0)
    sums = jnp.dot(table, stacked, preferred_element_type=jnp.float32)
    return folded(jnp.split(sums, 3, axis=0))


def multiplied(left, right):
    shifted = [left]
    for _ in range(2):
        shifted.append(reduced(shifted[-1] * 256.0))
    parts = [digits_of(part) for part in shifted]
    stacked_left = jnp.concatenate(
        [jnp.concatenate([part[digit] for part in parts], axis=2) for digit in range(3)], axis=1
    )
    stacked_right = jnp.concatenate(digits_of(right), axis=1)
    sums = jnp.einsum(
        "brk,bkc->brc", stacked_left, stacked_right, preferred_element_type=jnp.float32
    )
    return folded(jnp.split(sums, 3, axis=1))


def from_points(values):
    table = point_back_table(64)
    half = POINTS // 2
    total = 0.0
    for start in (0, half):
        total = total + transformed(
            jnp.asarray(stacked_table(table[:, start : start + half])), values[start : start + half]
        )
    total = reduced(total)
    return jnp.where(total < 0.0, total + float(modulus), total)


def shards(left_factor, right_factor):
    axes = ("deg", "row")
    blocks = lax.axis_size("deg")
    groups = lax.axis_size("row")
    rows = left_factor.shape[1]
    inner = right_factor.shape[1]
    flat = jnp.concatenate(
        [left_factor.reshape(BLOCK, rows * KD), right_factor.reshape(BLOCK, inner * CD)], axis=1
    )
    points = transformed(jnp.asarray(point_table()), flat)
    received = lax.all_to_all(points, axes, 0, 0, tiled=True)
    here = transformed(
        jnp.asarray(block_table(blocks)), received.reshape(blocks, groups * flat.shape[1])
    )
    here = here.reshape(2 * blocks, groups, flat.shape[1])
    left = here[:, :, : rows * KD].reshape(2 * blocks, groups * rows, KD)
    right = here[:, :, rows * KD :].reshape(2 * blocks, groups * inner, CD)
    product = multiplied(left, right).reshape(2 * blocks, groups * rows * CD)
    odd = lax.axis_index("row") % 2
    table = jnp.where(
        odd == 1,
        jnp.asarray(block_back_table(blocks, -1)),
        jnp.asarray(block_back_table(blocks, 1)),
    )
    back = transformed(table, product)
    back = back.reshape(blocks, 2, groups, rows * CD).transpose(0, 2, 1, 3)
    returned = lax.all_to_all(
        back.reshape(blocks * groups, 2 * rows * CD), axes, 0, 0, tiled=True
    )
    coeffs = from_points(returned)
    out = coeffs.reshape(BLOCK, 2, rows, CD).transpose(1, 0, 2, 3)
    return (out / modulus).reshape(2 * BLOCK, rows, CD)


def solution(mesh):
    placed = P("deg", "row", None)
    return jax.shard_map(
        shards, mesh=mesh, in_specs=(placed, placed), out_specs=placed, check_vma=False
    )
```

```python
import numpy as np
import jax
import jax.numpy as jnp
from jax import lax
from jax.experimental import pallas as pl
from jax.experimental.pallas import tpu as pltpu
from jax.sharding import PartitionSpec as P

modulus = 7340033
generator = 3
inverse_modulus = 1.0 / modulus
modulus_high = float(modulus - 1)

BLOCK = 256
POINTS = 2 * BLOCK
KD = 64
CD = 64


def powers(root, exponents, order):
    table = np.ones(order, np.int64)
    for position in range(1, order):
        table[position] = table[position - 1] * root % modulus
    return table[exponents % order]


def digit_rows(values):
    centred = np.where(values > modulus // 2, values - modulus, values)
    digits = []
    for _ in range(2):
        low = (centred + 128) % 256 - 128
        digits.append(low)
        centred = (centred - low) // 256
    digits.append(centred)
    return np.concatenate(digits, axis=0).astype(jnp.bfloat16)


MESH = pl.DeviceIdType.MESH
LANES = 128
BLOCKS = 64
LENGTH = 2 * BLOCKS
CHUNKS = 5
LINE = 8
PLANE = 64


def stacked_columns(values):
    return np.concatenate([values * 256**digit % modulus for digit in range(3)], axis=1)


def plane_order():
    place = np.arange(BLOCKS)
    core, rest = place // (BLOCKS // 2), place % (BLOCKS // 2)
    return rest * 2 + core


def point_table():
    root = pow(generator, (modulus - 1) // POINTS, modulus)
    exponents = np.arange(POINTS)[:, None] * np.arange(BLOCK)[None, :]
    rows = digit_rows(stacked_columns(powers(root, exponents, POINTS)))
    rows = rows.reshape(3, LINE, PLANE, 3 * BLOCK).transpose(1, 0, 2, 3)
    return rows.reshape(LINE, 3 * PLANE, 3 * BLOCK)


def block_table():
    root = pow(generator, (modulus - 1) // LENGTH, modulus)
    exponents = np.arange(LENGTH)[:, None] * plane_order()[None, :]
    return digit_rows(stacked_columns(powers(root, exponents, LENGTH)))


def block_back_table():
    root = pow(generator, (modulus - 1) // LENGTH, modulus)
    rows = np.concatenate([2 * plane_order() + half for half in range(2)])
    table = powers(root, -rows[:, None] * np.arange(LENGTH)[None, :], LENGTH)
    signed = []
    for sign in (1, -1):
        carry = 1 + sign * powers(root, np.arange(LENGTH), LENGTH)
        signed.append(digit_rows(stacked_columns(table * carry[None, :] % modulus)))
    return np.stack(signed)


def point_back_table():
    root = pow(generator, (modulus - 1) // POINTS, modulus)
    exponents = -np.arange(BLOCK)[:, None] * np.arange(POINTS)[None, :]
    scale = pow(2 * BLOCKS * POINTS, modulus - 2, modulus)
    table = powers(root, exponents, POINTS) * scale % modulus
    return np.stack(
        [digit_rows(stacked_columns(table[:, part : part + BLOCK])) for part in (0, BLOCK)]
    )


def lane_order():
    source = np.arange(LANES).reshape(2, 8, 2, 4).transpose(0, 2, 1, 3).reshape(LANES)
    matrix = np.zeros((LANES, LANES), np.float32)
    matrix[source, np.arange(LANES)] = 1.0
    return matrix.astype(jnp.bfloat16)


def reduced(values):
    quotient = jnp.round(values * inverse_modulus)
    return (values - quotient * modulus_high) - quotient


def folded(low, middle, high):
    return reduced(reduced((reduced(high * 256.0) + middle) * 256.0) + low)


def digits_of(values):
    high = jnp.round(values * (1.0 / 65536.0))
    rest = values - high * 65536.0
    middle = jnp.round(rest * (1.0 / 256.0))
    return [rest - middle * 256.0, middle, high]


def stacked_digits(values):
    return jnp.concatenate([digit.astype(jnp.bfloat16) for digit in digits_of(values)], axis=0)


def matmul(left, right):
    return jnp.dot(left, right, preferred_element_type=jnp.float32)


def thirds(sums):
    rows = sums.shape[0] // 3
    return [sums[part * rows : (part + 1) * rows] for part in range(3)]


def kernel(
    x_ref,
    lane_ref,
    point_ref,
    block_ref,
    back_ref,
    point_back_ref,
    out_ref,
    line_out,
    line_in,
    plane_out,
    plane_in,
    left_hat,
    right_hat,
    product_hat,
    line_send,
    line_recv,
    plane_send,
    plane_recv,
):
    deg = lax.axis_index("deg")
    row = lax.axis_index("row")
    core = lax.rem(deg, 2)
    z_lo = lax.rem(deg // 2, 4)
    y = deg // 8
    x = row // 2
    z_hi = lax.rem(row, 2)
    me_line = x * 2 + core
    me_plane = z_hi * 32 + y * 4 + z_lo

    def line_device(other):
        return (
            (y * 4 + z_lo) * 2 + lax.rem(other, 2),
            (other // 2) * 2 + z_hi,
        )

    def plane_device(other):
        return (
            (lax.rem(other // 4, 8) * 4 + lax.rem(other, 4)) * 2 + core,
            x * 2 + other // 32,
        )

    barrier = pltpu.get_barrier_semaphore()

    @pl.loop(1, LINE)
    def _(step):
        pl.semaphore_signal(
            barrier,
            inc=1,
            device_id=line_device(lax.rem(me_line + step, LINE)),
            device_id_type=MESH,
        )

    @pl.loop(1, PLANE)
    def _(step):
        pl.semaphore_signal(
            barrier,
            inc=1,
            device_id=plane_device(lax.rem(me_plane + step, PLANE)),
            device_id_type=MESH,
        )

    def line_rows(other):
        return pl.ds(pl.multiple_of(other * PLANE, PLANE), PLANE)

    def plane_rows(other):
        return pl.ds(pl.multiple_of(other * LINE, LINE), LINE)

    def line_copy(part, other):
        return pltpu.make_async_remote_copy(
            src_ref=line_out.at[part, line_rows(other)],
            dst_ref=line_in.at[part, line_rows(me_line)],
            send_sem=line_send.at[part],
            recv_sem=line_recv.at[part],
            device_id=line_device(other),
            device_id_type=MESH,
        )

    def plane_copy(part, other):
        return pltpu.make_async_remote_copy(
            src_ref=plane_out.at[part, plane_rows(other)],
            dst_ref=plane_in.at[part, plane_rows(me_plane)],
            send_sem=plane_send.at[part],
            recv_sem=plane_recv.at[part],
            device_id=plane_device(other),
            device_id_type=MESH,
        )

    def wait_line(part, semaphore):
        span = line_in.at[part, pl.ds(0, (LINE - 1) * PLANE)]
        pltpu.make_async_copy(span, span, semaphore.at[part]).wait()

    def wait_plane(part, semaphore):
        span = plane_in.at[part, pl.ds(0, (PLANE - 1) * LINE)]
        pltpu.make_async_copy(span, span, semaphore.at[part]).wait()

    def send_plane(part, make):
        @pl.loop(1, PLANE)
        def _(step):
            other = lax.rem(me_plane + step * PLANE_STRIDE, PLANE)
            if make is not None:
                plane_out[part, plane_rows(other)] = make(other)
            plane_copy(part, other).start()

        own = plane_out[part, plane_rows(me_plane)] if make is None else make(me_plane)
        plane_in[part, plane_rows(me_plane)] = own

    def send_line(part, make):
        @pl.loop(1, LINE)
        def _(step):
            other = lax.rem(me_line + step, LINE)
            if make is not None:
                line_out[part, line_rows(other)] = make(other)
            line_copy(part, other).start()

        own = line_out[part, line_rows(me_line)] if make is None else make(me_line)
        line_in[part, line_rows(me_line)] = own

    def line_to_plane(part):
        send_plane(part, lambda other: line_in[part, pl.ds(other, LINE, stride=PLANE), :])

    def plane_to_line(part):
        send_line(part, lambda other: plane_in[part, pl.ds(other, PLANE, stride=LINE), :])

    def points_of(part):
        stacked = stacked_digits(x_ref[part])
        if part == 0:
            stacked = matmul(stacked, lane_ref[...]).astype(jnp.bfloat16)

        def make(other):
            return folded(*thirds(matmul(point_ref[other], stacked)))

        return make

    first = points_of(0)

    @pl.loop(0, LINE)
    def _(other):
        plane_out[0, pl.ds(other, PLANE, stride=LINE), :] = first(other)

    pl.semaphore_wait(barrier, LINE + PLANE - 2)
    send_plane(0, None)
    for part in range(1, CHUNKS):
        send_line(part, points_of(part))
        if part >= 2:
            wait_line(part - 1, line_recv)
            line_to_plane(part - 1)
    wait_plane(0, plane_recv)
    plane_to_line(0)
    wait_line(CHUNKS - 1, line_recv)
    line_to_plane(CHUNKS - 1)

    def blocks_of(part, group):
        x_of, z_of = group // 2, lax.rem(group, 2)
        pieces = []
        for core_of in range(2):
            line = x_of * 2 + core_of
            if part == 0:
                start = pl.multiple_of(line * PLANE + z_of * 32, 32)
                pieces.append(line_in[part, pl.ds(start, 32), :])
            else:
                start = z_of * 32 * LINE + line
                pieces.append(plane_in[part, pl.ds(start, 32, stride=LINE), :])
        return jnp.concatenate(pieces, axis=0)

    def transform_blocks(part, store):
        @pl.loop(0, LINE // 2)
        def _(pair):
            wide = jnp.concatenate(
                [blocks_of(part, pair * 2), blocks_of(part, pair * 2 + 1)], axis=1
            )
            spectrum = folded(*thirds(matmul(block_ref[...], stacked_digits(wide))))
            store(pair * 2, spectrum[:, :LANES])
            store(pair * 2 + 1, spectrum[:, LANES:])

    def store_left(group, values):
        left_hat[pl.ds(group, LENGTH, stride=8), :] = values

    wait_line(0, line_recv)
    transform_blocks(0, store_left)
    for part in range(1, CHUNKS):

        def store_right(group, values):
            right_hat[pl.ds(group * 4 + (part - 1), LENGTH, stride=32), :] = values

        wait_plane(part, plane_recv)
        transform_blocks(part, store_right)

    batch = 8
    lane = lax.broadcasted_iota(jnp.int32, (8 * batch, LANES), 1)
    window = lane // 32
    low_half = lax.broadcasted_iota(jnp.int32, (8, LANES), 1) < 64

    @pl.loop(0, LENGTH // batch)
    def _(step):
        base = pl.multiple_of(step * 8 * batch, 8 * batch)
        left = left_hat[pl.ds(base, 8 * batch), :]
        factors = []
        for choice in range(4):
            spread = jnp.where(window == choice, left, 0.0)
            spread = spread + pltpu.roll(spread, 64, 1)
            spread = spread + pltpu.roll(spread, 32, 1)
            once = reduced(spread * 256.0)
            twice = reduced(once * 256.0)
            spread = jnp.where(window == 0, spread, jnp.where(window == 1, once, twice))
            factors.append(digits_of(jnp.where(window == 3, 0.0, spread)))
        for index in range(batch):
            rows = slice(8 * index, 8 * index + 8)
            stacked_left = jnp.concatenate(
                [digit[rows] for factor in factors for digit in factor], axis=0
            ).astype(jnp.bfloat16)
            start = pl.multiple_of((step * batch + index) * 32, 32)
            right = digits_of(right_hat[pl.ds(start, 32), :])
            stacked_right = jnp.concatenate(right + [right[2]], axis=0).astype(jnp.bfloat16)
            sums = matmul(stacked_left, stacked_right)
            parts = [
                [sums[24 * choice + 8 * digit : 24 * choice + 8 * digit + 8] for digit in range(3)]
                for choice in range(4)
            ]
            totals = [
                jnp.where(
                    low_half,
                    parts[0][digit] + pltpu.roll(parts[1][digit], 64, 1),
                    pltpu.roll(parts[2][digit], 64, 1) + parts[3][digit],
                )
                for digit in range(3)
            ]
            start = pl.multiple_of(base + 8 * index, 8)
            product_hat[pl.ds(start, 8), :] = folded(*totals)

    first_part, second_part = CHUNKS, CHUNKS + 1
    parity = lax.rem(z_lo, 2)

    @pl.loop(0, LINE // 2)
    def _(pair):
        wide = jnp.concatenate(
            [product_hat[pl.ds(pair * 2 + side, LENGTH, stride=8), :] for side in range(2)], axis=1
        )
        values = folded(*thirds(matmul(back_ref[parity], stacked_digits(wide))))
        for side in range(2):
            group = pair * 2 + side
            x_of, z_of = group // 2, lax.rem(group, 2)
            for core_of in range(2):
                line = x_of * 2 + core_of
                piece = values[32 * core_of : 32 * core_of + 32, LANES * side : LANES * side + LANES]
                plane_out[first_part, pl.ds(z_of * 32 * LINE + line, 32, stride=LINE), :] = piece
                piece = values[
                    64 + 32 * core_of : 96 + 32 * core_of, LANES * side : LANES * side + LANES
                ]
                start = pl.multiple_of(line * PLANE + z_of * 32, 32)
                line_out[second_part, pl.ds(start, 32), :] = piece

    send_line(second_part, None)
    send_plane(first_part, None)
    wait_line(second_part, line_recv)
    line_to_plane(second_part)
    wait_plane(first_part, plane_recv)
    plane_to_line(first_part)

    def coefficients(half, load):
        total = None
        for side in range(2):
            values = jnp.concatenate([load(side * 4 + line) for line in range(4)], axis=0)
            sums = folded(*thirds(matmul(point_back_ref[side], stacked_digits(values))))
            total = sums if total is None else reduced(total + sums)
        out_ref[half] = jnp.where(total < 0.0, total + float(modulus), total)

    wait_line(first_part, line_recv)
    coefficients(0, lambda line: line_in[first_part, pl.ds(line * PLANE, PLANE), :])
    wait_plane(second_part, plane_recv)
    coefficients(1, lambda line: plane_in[second_part, pl.ds(line, PLANE, stride=LINE), :])

    for part in range(CHUNKS + 2):
        wait_line(part, line_send)
        wait_plane(part, plane_send)


PLANE_STRIDE = 1


def shards(left_factor, right_factor):
    local, rows, depth = left_factor.shape
    left = left_factor.reshape(1, local, rows * depth)
    right = right_factor.reshape(local, 2, 4, CD).transpose(2, 0, 1, 3).reshape(4, local, 2 * CD)
    columns = jnp.concatenate([left, right], axis=0)
    parts = CHUNKS + 2
    whole = pl.BlockSpec(memory_space=pltpu.VMEM)
    buffer = pltpu.VMEM((parts, POINTS, LANES), jnp.float32)
    semaphores = pltpu.SemaphoreType.DMA((parts,))
    coeffs = pl.pallas_call(
        kernel,
        out_shape=jax.ShapeDtypeStruct((2, BLOCK, LANES), jnp.float32),
        in_specs=[whole] * 6,
        out_specs=whole,
        scratch_shapes=[buffer] * 4
        + [
            pltpu.VMEM((LENGTH * 8, LANES), jnp.float32),
            pltpu.VMEM((LENGTH * 32, LANES), jnp.float32),
            pltpu.VMEM((LENGTH * 8, LANES), jnp.float32),
        ]
        + [semaphores] * 4,
        compiler_params=pltpu.CompilerParams(
            collective_id=0, has_side_effects=True, vmem_limit_bytes=56 * 2**20
        ),
    )(
        columns,
        jnp.asarray(lane_order()),
        jnp.asarray(point_table()),
        jnp.asarray(block_table()),
        jnp.asarray(block_back_table()),
        jnp.asarray(point_back_table()),
    )
    return (coeffs / modulus).reshape(2 * local, rows, CD)


def solution(mesh):
    placed = P("deg", "row", None)
    return jax.shard_map(
        shards, mesh=mesh, in_specs=(placed, placed), out_specs=placed, check_vma=False
    )
```

```python
import numpy as np
import jax
import jax.numpy as jnp
from jax import lax
from jax.experimental import pallas as pl
from jax.experimental.pallas import tpu as pltpu
from jax.sharding import PartitionSpec as P

modulus = 7340033
generator = 3
inverse_modulus = 1.0 / modulus
modulus_high = float(modulus - 1)

BLOCK = 256
POINTS = 2 * BLOCK
KD = 64
CD = 64


def powers(root, exponents, order):
    table = np.ones(order, np.int64)
    for position in range(1, order):
        table[position] = table[position - 1] * root % modulus
    return table[exponents % order]


def digit_rows(values):
    centred = np.where(values > modulus // 2, values - modulus, values)
    digits = []
    for _ in range(2):
        low = (centred + 128) % 256 - 128
        digits.append(low)
        centred = (centred - low) // 256
    digits.append(centred)
    return np.concatenate(digits, axis=0).astype(jnp.bfloat16)


MESH = pl.DeviceIdType.MESH
LANES = 128
BLOCKS = 64
LENGTH = 2 * BLOCKS
CHUNKS = 5
LINE = 8
PLANE = 64


def stacked_columns(values):
    return np.concatenate([values * 256**digit % modulus for digit in range(3)], axis=1)


def block_order():
    place = np.arange(BLOCKS)
    return place % LINE * LINE + place // LINE


def point_table():
    root = pow(generator, (modulus - 1) // POINTS, modulus)
    exponents = np.arange(POINTS)[:, None] * np.arange(BLOCK)[None, :]
    rows = digit_rows(stacked_columns(powers(root, exponents, POINTS)))
    rows = rows.reshape(3, LINE, PLANE, 3 * BLOCK).transpose(1, 0, 2, 3)
    return rows.reshape(LINE, 3 * PLANE, 3 * BLOCK)


def block_table():
    root = pow(generator, (modulus - 1) // LENGTH, modulus)
    exponents = np.arange(LENGTH)[:, None] * block_order()[None, :]
    return digit_rows(stacked_columns(powers(root, exponents, LENGTH)))


def block_back_table():
    root = pow(generator, (modulus - 1) // LENGTH, modulus)
    rows = np.concatenate([2 * block_order(), 2 * np.arange(BLOCKS) + 1])
    table = powers(root, -rows[:, None] * np.arange(LENGTH)[None, :], LENGTH)
    signed = []
    for sign in (1, -1):
        carry = 1 + sign * powers(root, np.arange(LENGTH), LENGTH)
        signed.append(digit_rows(stacked_columns(table * carry[None, :] % modulus)))
    return np.stack(signed)


def point_back_table():
    root = pow(generator, (modulus - 1) // POINTS, modulus)
    exponents = -np.arange(BLOCK)[:, None] * np.arange(POINTS)[None, :]
    scale = pow(2 * BLOCKS * POINTS, modulus - 2, modulus)
    table = powers(root, exponents, POINTS) * scale % modulus
    return np.stack(
        [digit_rows(stacked_columns(table[:, part : part + BLOCK])) for part in (0, BLOCK)]
    )


def row_order():
    source = np.arange(LANES).reshape(2, 8, 4, 2).transpose(0, 3, 1, 2).reshape(LANES)
    matrix = np.zeros((LANES, LANES), np.float32)
    matrix[np.arange(LANES), source] = 1.0
    return matrix.astype(jnp.bfloat16)


def reduced(values):
    quotient = jnp.round(values * inverse_modulus)
    return (values - quotient * modulus_high) - quotient


def folded(low, middle, high):
    return reduced(reduced((reduced(high * 256.0) + middle) * 256.0) + low)


def digits_of(values):
    high = jnp.round(values * (1.0 / 65536.0))
    rest = values - high * 65536.0
    middle = jnp.round(rest * (1.0 / 256.0))
    return [rest - middle * 256.0, middle, high]


def stacked_digits(values, axis=0):
    return jnp.concatenate([digit.astype(jnp.bfloat16) for digit in digits_of(values)], axis=axis)


def matmul(left, right):
    return jnp.dot(left, right, preferred_element_type=jnp.float32)


def matmul_transposed(left, right):
    return lax.dot_general(
        left, right, (((1,), (1,)), ((), ())), preferred_element_type=jnp.float32
    )


def thirds(sums):
    rows = sums.shape[0] // 3
    return [sums[part * rows : (part + 1) * rows] for part in range(3)]


def kernel(
    left_ref,
    right_ref,
    order_ref,
    point_ref,
    block_hbm,
    back_hbm,
    point_back_hbm,
    out_ref,
    block_ref,
    back_ref,
    point_back_ref,
    line_out,
    line_in,
    plane_out,
    plane_in,
    left_hat,
    left_digits,
    right_hat,
    product_hat,
    table_sem,
    line_send,
    line_recv,
    plane_send,
    plane_recv,
):
    deg = lax.axis_index("deg")
    row = lax.axis_index("row")
    rest = lax.rem(deg, 8)
    me_line = deg // 8
    me_plane = row * 8 + rest

    def line_device(other):
        return (other * 8 + rest, row)

    def plane_device(other):
        return (me_line * 8 + lax.rem(other, 8), other // 8)

    barrier = pltpu.get_barrier_semaphore()

    @pl.loop(1, LINE)
    def _(step):
        pl.semaphore_signal(
            barrier,
            inc=1,
            device_id=line_device(lax.rem(me_line + step, LINE)),
            device_id_type=MESH,
        )

    @pl.loop(1, PLANE)
    def _(step):
        pl.semaphore_signal(
            barrier,
            inc=1,
            device_id=plane_device(lax.rem(me_plane + step, PLANE)),
            device_id_type=MESH,
        )

    tables = [
        pltpu.make_async_copy(source, target, table_sem.at[index])
        for index, (source, target) in enumerate(
            [(block_hbm, block_ref), (back_hbm, back_ref), (point_back_hbm, point_back_ref)]
        )
    ]
    for table in tables:
        table.start()

    def line_rows(other):
        return pl.ds(pl.multiple_of(other * PLANE, PLANE), PLANE)

    def plane_rows(other):
        return pl.ds(pl.multiple_of(other * LINE, LINE), LINE)

    def line_copy(part, other):
        return pltpu.make_async_remote_copy(
            src_ref=line_out.at[part, line_rows(other)],
            dst_ref=line_in.at[part, line_rows(me_line)],
            send_sem=line_send.at[part],
            recv_sem=line_recv.at[part],
            device_id=line_device(other),
            device_id_type=MESH,
        )

    def plane_copy(part, other):
        return pltpu.make_async_remote_copy(
            src_ref=plane_out.at[part, plane_rows(other)],
            dst_ref=plane_in.at[part, plane_rows(me_plane)],
            send_sem=plane_send.at[part],
            recv_sem=plane_recv.at[part],
            device_id=plane_device(other),
            device_id_type=MESH,
        )

    def wait_line(part, semaphore):
        span = line_in.at[part, pl.ds(0, (LINE - 1) * PLANE)]
        pltpu.make_async_copy(span, span, semaphore.at[part]).wait()

    def wait_plane(part, semaphore):
        span = plane_in.at[part, pl.ds(0, (PLANE - 1) * LINE)]
        pltpu.make_async_copy(span, span, semaphore.at[part]).wait()

    def far_first(step):
        half = step // 2
        odd = lax.rem(step, 2)
        return odd * (3 - half) + (1 - odd) * (4 + half)

    def plane_partner(step):
        outer = step // 8
        pair = outer // 2
        odd = lax.rem(pair, 2)
        shift = odd * (1 - pair // 2) + (1 - odd) * (2 + pair // 2)
        x_other = lax.rem(row // 2 + shift, 4)
        z_here = lax.rem(row, 2) * 4 + rest // 2
        z_other = lax.rem(z_here + far_first(lax.rem(step, 8)), 8)
        core_other = lax.rem(rest + 1 - lax.rem(outer, 2), 2)
        row_other = x_other * 2 + z_other // 4
        return row_other * 8 + lax.rem(z_other, 4) * 2 + core_other

    def send_plane(part, make):
        @pl.loop(0, PLANE - 1, unroll=PLANE_UNROLL)
        def _(step):
            other = plane_partner(step)
            if make is not None:
                plane_out[part, plane_rows(other)] = make(other)
            plane_copy(part, other).start()

        own = plane_out[part, plane_rows(me_plane)] if make is None else make(me_plane)
        plane_in[part, plane_rows(me_plane)] = own

    def send_line(part, make):
        @pl.loop(0, LINE - 1, unroll=LINE - 1)
        def _(step):
            other = lax.rem(me_line + far_first(step), LINE)
            if make is not None:
                line_out[part, line_rows(other)] = make(other)
            line_copy(part, other).start()

        own = line_out[part, line_rows(me_line)] if make is None else make(me_line)
        line_in[part, line_rows(me_line)] = own

    def line_to_plane(part):
        send_plane(part, lambda other: line_in[part, pl.ds(other, LINE, stride=PLANE), :])

    def plane_to_line(part):
        send_line(part, lambda other: plane_in[part, pl.ds(other, PLANE, stride=LINE), :])

    def right_digits(first, count):
        return stacked_digits(right_ref[pl.ds((first - 1) * LANES, count * LANES), :], axis=1)

    def points_of(other, stacked):
        return folded(*thirds(matmul_transposed(point_ref[other], stacked)))

    left = stacked_digits(left_ref[...], axis=1)
    left = matmul(order_ref[...], left).astype(jnp.bfloat16)
    stacked = jnp.concatenate([left, right_digits(1, 1)], axis=0)

    @pl.loop(0, LINE, unroll=POINT_UNROLL)
    def _(other):
        values = points_of(other, stacked)
        plane_out[0, pl.ds(other, PLANE, stride=LINE), :] = values[:, :LANES]
        line_out[1, line_rows(other), :] = values[:, LANES:]

    pl.semaphore_wait(barrier, LINE + PLANE - 2)
    send_line(1, None)
    send_plane(0, None)

    stacked_more = right_digits(2, 2)

    @pl.loop(0, LINE, unroll=POINT_UNROLL)
    def _(other):
        values = points_of(other, stacked_more)
        plane_out[2, pl.ds(other, PLANE, stride=LINE), :] = values[:, :LANES]
        line_out[3, line_rows(other), :] = values[:, LANES:]

    send_line(3, None)
    wait_line(1, line_recv)
    line_to_plane(1)

    stacked_last = right_digits(4, 1)

    @pl.loop(0, LINE, unroll=POINT_UNROLL)
    def _(other):
        line_out[4, line_rows(other), :] = points_of(other, stacked_last)

    wait_plane(0, plane_recv)
    plane_to_line(0)
    send_line(4, None)
    send_plane(2, None)
    wait_line(3, line_recv)
    line_to_plane(3)

    def blocks_of(part, group):
        if part in (0, 2):
            return jnp.concatenate(
                [
                    line_in[part, pl.ds(group * LINE + index, LINE, stride=PLANE), :]
                    for index in range(LINE)
                ],
                axis=0,
            )
        return plane_in[part, pl.ds(pl.multiple_of(group * PLANE, PLANE), PLANE), :]

    def transform_blocks(part):
        @pl.loop(0, LINE // 2, unroll=BLOCK_UNROLL)
        def _(pair):
            wide = jnp.concatenate(
                [blocks_of(part, pair * 2), blocks_of(part, pair * 2 + 1)], axis=1
            )
            spectrum = folded(*thirds(matmul(block_ref[...], stacked_digits(wide))))
            for side in range(2):
                group = pair * 2 + side
                values = spectrum[:, LANES * side : LANES * side + LANES]
                if part == 0:
                    left_hat[pl.ds(group, LENGTH, stride=8), :] = values
                else:
                    right_hat[pl.ds(group * 4 + part - 1, LENGTH, stride=32), :] = values

    batch = 8
    lane = lax.broadcasted_iota(jnp.int32, (8 * batch, LANES), 1)
    window = lane // 32
    low_half = lax.broadcasted_iota(jnp.int32, (8, LANES), 1) < 64

    def prepare_left():
        @pl.loop(0, LENGTH // batch, unroll=LEFT_UNROLL)
        def _(step):
            base = pl.multiple_of(step * 8 * batch, 8 * batch)
            left = left_hat[pl.ds(base, 8 * batch), :]
            factors = []
            for choice in range(4):
                spread = jnp.where(window == choice, left, 0.0)
                for shift in (64, 32):
                    spread = spread + pltpu.roll(spread, shift, 1)
                once = reduced(spread * 256.0)
                twice = reduced(once * 256.0)
                spread = jnp.where(window == 0, spread, jnp.where(window == 1, once, twice))
                factors.append(digits_of(jnp.where(window < 3, spread, 0.0)))
            for index in range(batch):
                rows = slice(8 * index, 8 * index + 8)
                start = pl.multiple_of((step * batch + index) * 96, 96)
                left_digits[pl.ds(start, 96), :] = jnp.concatenate(
                    [digit[rows] for factor in factors for digit in factor], axis=0
                ).astype(jnp.bfloat16)

    def multiply():
        @pl.loop(0, LENGTH // batch, unroll=PRODUCT_UNROLL)
        def _(step):
            for index in range(batch):
                place = step * batch + index
                left = left_digits[pl.ds(pl.multiple_of(place * 96, 96), 96), :]
                right = digits_of(right_hat[pl.ds(pl.multiple_of(place * 32, 32), 32), :])
                right = jnp.concatenate(right + [right[2]], axis=0).astype(jnp.bfloat16)
                sums = matmul(left, right)
                parts = [sums[8 * part : 8 * part + 8] for part in range(12)]
                totals = [
                    jnp.where(low_half, parts[digit], parts[9 + digit])
                    + pltpu.roll(jnp.where(low_half, parts[6 + digit], parts[3 + digit]), 64, 1)
                    for digit in range(3)
                ]
                product_hat[pl.ds(pl.multiple_of(place * 8, 8), 8), :] = folded(*totals)

    tables[0].wait()
    wait_plane(1, plane_recv)
    transform_blocks(1)
    wait_line(0, line_recv)
    transform_blocks(0)
    wait_plane(2, plane_recv)
    plane_to_line(2)
    wait_line(4, line_recv)
    line_to_plane(4)
    prepare_left()
    wait_plane(3, plane_recv)
    transform_blocks(3)
    wait_line(2, line_recv)
    transform_blocks(2)
    wait_plane(4, plane_recv)
    transform_blocks(4)
    multiply()

    first_part, second_part = CHUNKS, CHUNKS + 1
    parity = lax.rem(rest, 2)
    tables[1].wait()

    @pl.loop(0, LINE // 2, unroll=BLOCK_UNROLL)
    def _(pair):
        wide = jnp.concatenate(
            [product_hat[pl.ds(pair * 2 + side, LENGTH, stride=8), :] for side in range(2)], axis=1
        )
        values = folded(*thirds(matmul(back_ref[parity], stacked_digits(wide))))
        for side in range(2):
            group = pair * 2 + side
            mine = values[:, LANES * side : LANES * side + LANES]
            plane_out[first_part, pl.ds(pl.multiple_of(group * PLANE, PLANE), PLANE), :] = mine[:PLANE]
            for line in range(LINE):
                start = pl.multiple_of(line * PLANE + group * LINE, LINE)
                line_out[second_part, pl.ds(start, LINE), :] = mine[
                    PLANE + LINE * line : PLANE + LINE * line + LINE
                ]

    send_line(second_part, None)
    send_plane(first_part, None)
    wait_line(second_part, line_recv)
    line_to_plane(second_part)
    wait_plane(first_part, plane_recv)
    plane_to_line(first_part)

    def coefficients(half, load):
        total = None
        for side in range(2):
            values = jnp.concatenate([load(side * 4 + line) for line in range(4)], axis=0)
            sums = folded(*thirds(matmul(point_back_ref[side], stacked_digits(values))))
            total = sums if total is None else reduced(total + sums)
        total = jnp.where(total < 0.0, total + float(modulus), total)
        out_ref[:, half * BLOCK : half * BLOCK + BLOCK] = (total / float(modulus)).T

    tables[2].wait()
    wait_line(first_part, line_recv)
    coefficients(0, lambda line: line_in[first_part, pl.ds(line * PLANE, PLANE), :])
    wait_plane(second_part, plane_recv)
    coefficients(1, lambda line: plane_in[second_part, pl.ds(line, PLANE, stride=LINE), :])

    for part in range(CHUNKS + 2):
        wait_line(part, line_send)
        wait_plane(part, plane_send)


PLANE_UNROLL = 7
POINT_UNROLL = 2
BLOCK_UNROLL = 2
LEFT_UNROLL = 2
PRODUCT_UNROLL = 4


def shards(left_factor, right_factor):
    local, rows, depth = left_factor.shape
    left = left_factor.transpose(1, 2, 0).reshape(LANES, local)
    right = right_factor.transpose(1, 2, 0).reshape((CHUNKS - 1) * LANES, local)
    parts = CHUNKS + 2
    whole = pl.BlockSpec(memory_space=pltpu.VMEM)
    remote = pl.BlockSpec(memory_space=pl.ANY)
    buffer = pltpu.VMEM((parts, POINTS, LANES), jnp.float32)
    semaphores = pltpu.SemaphoreType.DMA((parts,))
    block, back, point_back = block_table(), block_back_table(), point_back_table()
    coeffs = pl.pallas_call(
        kernel,
        out_shape=jax.ShapeDtypeStruct((LANES, POINTS), jnp.float32),
        in_specs=[whole] * 4 + [remote] * 3,
        out_specs=whole,
        scratch_shapes=[
            pltpu.VMEM(table.shape, jnp.bfloat16) for table in (block, back, point_back)
        ]
        + [buffer] * 4
        + [
            pltpu.VMEM((LENGTH * 8, LANES), jnp.float32),
            pltpu.VMEM((LENGTH * 96, LANES), jnp.bfloat16),
            pltpu.VMEM((LENGTH * 32, LANES), jnp.float32),
            pltpu.VMEM((LENGTH * 8, LANES), jnp.float32),
        ]
        + [pltpu.SemaphoreType.DMA((3,))]
        + [semaphores] * 4,
        compiler_params=pltpu.CompilerParams(
            collective_id=0, has_side_effects=True, vmem_limit_bytes=56 * 2**20
        ),
    )(
        left,
        right,
        jnp.asarray(row_order()),
        jnp.asarray(point_table()),
        jnp.asarray(block),
        jnp.asarray(back),
        jnp.asarray(point_back),
    )
    return coeffs.reshape(rows, CD, 2 * local).transpose(2, 0, 1)


def solution(mesh):
    placed = P("deg", "row", None)
    return jax.shard_map(
        shards, mesh=mesh, in_specs=(placed, placed), out_specs=placed, check_vma=False
    )
```

```python
import numpy as np
import jax
import jax.numpy as jnp
from jax import lax
from jax.experimental import pallas as pl
from jax.experimental.pallas import tpu as pltpu
from jax.sharding import PartitionSpec as P

modulus = 7340033
generator = 3
inverse_modulus = 1.0 / modulus
modulus_high = float(modulus - 1)

BLOCK = 256
POINTS = 2 * BLOCK
KD = 64
CD = 64


def powers(root, exponents, order):
    table = np.ones(order, np.int64)
    for position in range(1, order):
        table[position] = table[position - 1] * root % modulus
    return table[exponents % order]


def digit_rows(values):
    centred = np.where(values > modulus // 2, values - modulus, values)
    digits = []
    for _ in range(2):
        low = (centred + 128) % 256 - 128
        digits.append(low)
        centred = (centred - low) // 256
    digits.append(centred)
    return np.concatenate(digits, axis=0).astype(jnp.bfloat16)


MESH = pl.DeviceIdType.MESH
LANES = 128
BLOCKS = 64
LENGTH = 2 * BLOCKS
CHUNKS = 5
LINE = 8
PLANE = 64


def stacked_columns(values):
    return np.concatenate([values * 256**digit % modulus for digit in range(3)], axis=1)


def block_order():
    return np.arange(BLOCKS).reshape(8, 4, 2).transpose(2, 1, 0).reshape(BLOCKS)


def point_table():
    root = pow(generator, (modulus - 1) // POINTS, modulus)
    exponents = np.arange(POINTS)[:, None] * np.arange(BLOCK)[None, :]
    rows = digit_rows(stacked_columns(powers(root, exponents, POINTS)))
    rows = rows.reshape(3, LINE, PLANE, 3 * BLOCK).transpose(1, 0, 2, 3)
    return rows.reshape(LINE, 3 * PLANE, 3 * BLOCK)


def block_table():
    root = pow(generator, (modulus - 1) // LENGTH, modulus)
    exponents = np.arange(LENGTH)[:, None] * block_order()[None, :]
    return digit_rows(stacked_columns(powers(root, exponents, LENGTH)))


def block_back_table():
    root = pow(generator, (modulus - 1) // LENGTH, modulus)
    rows = np.concatenate([2 * block_order(), 2 * block_order() + 1])
    table = powers(root, -rows[:, None] * np.arange(LENGTH)[None, :], LENGTH)
    signed = []
    for sign in (1, -1):
        carry = 1 + sign * powers(root, np.arange(LENGTH), LENGTH)
        signed.append(digit_rows(stacked_columns(table * carry[None, :] % modulus)))
    return np.stack(signed)


def point_back_table():
    root = pow(generator, (modulus - 1) // POINTS, modulus)
    exponents = -np.arange(BLOCK)[:, None] * np.arange(POINTS)[None, :]
    scale = pow(2 * BLOCKS * POINTS, modulus - 2, modulus)
    table = powers(root, exponents, POINTS) * scale % modulus
    return np.stack(
        [digit_rows(stacked_columns(table[:, part : part + BLOCK])) for part in (0, BLOCK)]
    )


def row_order():
    source = np.arange(LANES).reshape(2, 8, 4, 2).transpose(0, 3, 1, 2).reshape(LANES)
    matrix = np.zeros((LANES, LANES), np.float32)
    matrix[np.arange(LANES), source] = 1.0
    return matrix.astype(jnp.bfloat16)


def reduced(values):
    quotient = jnp.round(values * inverse_modulus)
    return (values - quotient * modulus_high) - quotient


def folded(low, middle, high):
    return reduced(reduced((reduced(high * 256.0) + middle) * 256.0) + low)


def digits_of(values):
    high = jnp.round(values * (1.0 / 65536.0))
    rest = values - high * 65536.0
    middle = jnp.round(rest * (1.0 / 256.0))
    return [rest - middle * 256.0, middle, high]


def stacked_digits(values, axis=0):
    return jnp.concatenate([digit.astype(jnp.bfloat16) for digit in digits_of(values)], axis=axis)


def matmul(left, right):
    return jnp.dot(left, right, preferred_element_type=jnp.float32)


def matmul_transposed(left, right):
    return lax.dot_general(
        left, right, (((1,), (1,)), ((), ())), preferred_element_type=jnp.float32
    )


def thirds(sums):
    rows = sums.shape[0] // 3
    return [sums[part * rows : (part + 1) * rows] for part in range(3)]


def kernel(
    left_ref,
    right_ref,
    order_ref,
    point_hbm,
    block_hbm,
    back_hbm,
    point_back_hbm,
    out_ref,
    point_ref,
    block_ref,
    back_ref,
    point_back_ref,
    line_out,
    line_in,
    plane_out,
    plane_in,
    left_hat,
    left_digits,
    right_hat,
    product_hat,
    point_sem,
    table_sem,
    line_send,
    line_recv,
    plane_send,
    plane_recv,
):
    deg = lax.axis_index("deg")
    row = lax.axis_index("row")
    rest = lax.rem(deg, 8)
    me_line = deg // 8
    core = lax.rem(rest, 2)
    z_lo = rest // 2
    me_plane = core * 32 + row * 4 + z_lo

    def point_copy(other):
        return pltpu.make_async_copy(point_hbm.at[other], point_ref.at[other], point_sem.at[other])

    for other in range(LINE):
        point_copy(other).start()

    def line_device(other):
        return (other * 8 + rest, row)

    def plane_device(other):
        device = me_line * 8 + lax.rem(other, 4) * 2 + other // 32
        return (device, lax.rem(other // 4, 8))

    barrier = pltpu.get_barrier_semaphore()

    @pl.loop(1, LINE, unroll=LINE - 1)
    def _(step):
        pl.semaphore_signal(
            barrier,
            inc=1,
            device_id=line_device(lax.rem(me_line + step, LINE)),
            device_id_type=MESH,
        )

    @pl.loop(1, PLANE, unroll=PLANE_UNROLL)
    def _(step):
        pl.semaphore_signal(
            barrier,
            inc=1,
            device_id=plane_device(lax.rem(me_plane + step, PLANE)),
            device_id_type=MESH,
        )

    tables = [
        pltpu.make_async_copy(source, target, table_sem.at[index])
        for index, (source, target) in enumerate(
            [(block_hbm, block_ref), (back_hbm, back_ref), (point_back_hbm, point_back_ref)]
        )
    ]
    for table in tables:
        table.start()

    def line_rows(other):
        return pl.ds(pl.multiple_of(other * PLANE, PLANE), PLANE)

    def plane_rows(other):
        return pl.ds(pl.multiple_of(other * LINE, LINE), LINE)

    def line_copy(part, other):
        return pltpu.make_async_remote_copy(
            src_ref=line_out.at[part, line_rows(other)],
            dst_ref=line_in.at[part, line_rows(me_line)],
            send_sem=line_send.at[part],
            recv_sem=line_recv.at[part],
            device_id=line_device(other),
            device_id_type=MESH,
        )

    def plane_copy(part, other):
        return pltpu.make_async_remote_copy(
            src_ref=plane_out.at[part, plane_rows(other)],
            dst_ref=plane_in.at[part, plane_rows(me_plane)],
            send_sem=plane_send.at[part],
            recv_sem=plane_recv.at[part],
            device_id=plane_device(other),
            device_id_type=MESH,
        )

    def wait_line(part, semaphore):
        span = line_in.at[part, pl.ds(0, (LINE - 1) * PLANE)]
        pltpu.make_async_copy(span, span, semaphore.at[part]).wait()

    def wait_plane(part, semaphore):
        span = plane_in.at[part, pl.ds(0, (PLANE - 1) * LINE)]
        pltpu.make_async_copy(span, span, semaphore.at[part]).wait()

    def far_first(step):
        half = step // 2
        odd = lax.rem(step, 2)
        return odd * (3 - half) + (1 - odd) * (4 + half)

    def core_partner(step, core_other):
        pair = step // 8
        odd = lax.rem(pair, 2)
        shift = odd * (1 - pair // 2) + (1 - odd) * (2 + pair // 2)
        x_other = lax.rem(row // 2 + shift, 4)
        z_here = lax.rem(row, 2) * 4 + z_lo
        z_other = lax.rem(z_here + far_first(lax.rem(step, 8)), 8)
        return core_other * 32 + (x_other * 2 + z_other // 4) * 4 + lax.rem(z_other, 4)

    def plane_partner(step):
        outer = step // 8
        core_other = lax.rem(core + 1 - lax.rem(outer, 2), 2)
        return core_partner(outer // 2 * 8 + lax.rem(step, 8), core_other)

    def send_plane(part, make):
        @pl.loop(0, PLANE - 1, unroll=PLANE_UNROLL)
        def _(step):
            other = plane_partner(step)
            if make is not None:
                plane_out[part, plane_rows(other)] = make(other)
            plane_copy(part, other).start()

        own = plane_out[part, plane_rows(me_plane)] if make is None else make(me_plane)
        plane_in[part, plane_rows(me_plane)] = own

    def send_line(part, make):
        @pl.loop(0, LINE - 1, unroll=LINE - 1)
        def _(step):
            other = lax.rem(me_line + far_first(step), LINE)
            if make is not None:
                line_out[part, line_rows(other)] = make(other)
            line_copy(part, other).start()

        own = line_out[part, line_rows(me_line)] if make is None else make(me_line)
        line_in[part, line_rows(me_line)] = own

    def line_to_plane(part):
        send_plane(part, lambda other: line_in[part, pl.ds(other, LINE, stride=PLANE), :])

    def plane_to_line(part):
        send_line(part, lambda other: plane_in[part, pl.ds(other, PLANE, stride=LINE), :])

    def right_digits(first, count):
        return stacked_digits(right_ref[pl.ds((first - 1) * LANES, count * LANES), :], axis=1)

    def points_of(other, stacked):
        return folded(*thirds(matmul_transposed(point_ref[other], stacked)))

    left = stacked_digits(left_ref[...], axis=1)
    left = matmul(order_ref[...], left).astype(jnp.bfloat16)
    stacked = jnp.concatenate([left, right_digits(1, 1)], axis=0)

    @pl.loop(0, LINE, unroll=POINT_UNROLL)
    def _(other):
        point_copy(other).wait()
        values = points_of(other, stacked)
        plane_out[0, pl.ds(other, PLANE, stride=LINE), :] = values[:, :LANES]
        line_out[1, line_rows(other), :] = values[:, LANES:]

    pl.semaphore_wait(barrier, LINE + PLANE - 2)
    send_line(1, None)
    send_plane(0, None)

    stacked_more = right_digits(2, 2)

    @pl.loop(0, LINE, unroll=POINT_UNROLL)
    def _(other):
        values = points_of(other, stacked_more)
        plane_out[2, pl.ds(other, PLANE, stride=LINE), :] = values[:, :LANES]
        line_out[3, line_rows(other), :] = values[:, LANES:]

    send_line(3, None)
    send_plane(2, None)

    stacked_last = right_digits(4, 1)

    @pl.loop(0, LINE, unroll=POINT_UNROLL)
    def _(other):
        line_out[4, line_rows(other), :] = points_of(other, stacked_last)

    send_line(4, None)
    wait_line(1, line_recv)
    line_to_plane(1)
    wait_plane(0, plane_recv)
    plane_to_line(0)
    wait_line(3, line_recv)
    line_to_plane(3)
    wait_plane(2, plane_recv)
    plane_to_line(2)
    wait_line(4, line_recv)
    line_to_plane(4)

    def blocks_of(part, group):
        if part in (0, 2):
            return jnp.concatenate(
                [
                    line_in[part, pl.ds(group * 4 + index // 4 * 32 + index % 4, 8, stride=64), :]
                    for index in range(LINE)
                ],
                axis=0,
            )
        return jnp.concatenate(
            [
                plane_in[part, pl.ds(pl.multiple_of(side * 256 + group * 32, 32), 32), :]
                for side in range(2)
            ],
            axis=0,
        )

    def transform_blocks(part):
        @pl.loop(0, LINE // 2, unroll=BLOCK_UNROLL)
        def _(pair):
            wide = jnp.concatenate(
                [blocks_of(part, pair * 2), blocks_of(part, pair * 2 + 1)], axis=1
            )
            spectrum = folded(*thirds(matmul(block_ref[...], stacked_digits(wide))))
            for side in range(2):
                group = pair * 2 + side
                values = spectrum[:, LANES * side : LANES * side + LANES]
                if part == 0:
                    left_hat[pl.ds(group, LENGTH, stride=8), :] = values
                else:
                    right_hat[pl.ds(group * 4 + part - 1, LENGTH, stride=32), :] = values

    batch = 8
    lane = lax.broadcasted_iota(jnp.int32, (8 * batch, LANES), 1)
    window = lane // 32
    low_half = lax.broadcasted_iota(jnp.int32, (8, LANES), 1) < 64

    def prepare_left():
        @pl.loop(0, LENGTH // batch, unroll=LEFT_UNROLL)
        def _(step):
            base = pl.multiple_of(step * 8 * batch, 8 * batch)
            left = left_hat[pl.ds(base, 8 * batch), :]
            factors = []
            for choice in range(4):
                spread = jnp.where(window == choice, left, 0.0)
                for shift in (64, 32):
                    spread = spread + pltpu.roll(spread, shift, 1)
                once = reduced(spread * 256.0)
                twice = reduced(once * 256.0)
                spread = jnp.where(window == 0, spread, jnp.where(window == 1, once, twice))
                factors.append(digits_of(jnp.where(window < 3, spread, 0.0)))
            for index in range(batch):
                rows = slice(8 * index, 8 * index + 8)
                start = pl.multiple_of((step * batch + index) * 96, 96)
                left_digits[pl.ds(start, 96), :] = jnp.concatenate(
                    [digit[rows] for factor in factors for digit in factor], axis=0
                ).astype(jnp.bfloat16)

    def multiply():
        @pl.loop(0, LENGTH // batch, unroll=PRODUCT_UNROLL)
        def _(step):
            for index in range(batch):
                place = step * batch + index
                left = left_digits[pl.ds(pl.multiple_of(place * 96, 96), 96), :]
                right = digits_of(right_hat[pl.ds(pl.multiple_of(place * 32, 32), 32), :])
                right = jnp.concatenate(right + [right[2]], axis=0).astype(jnp.bfloat16)
                sums = matmul(left, right)
                parts = [sums[8 * part : 8 * part + 8] for part in range(12)]
                totals = [
                    jnp.where(low_half, parts[digit], parts[9 + digit])
                    + pltpu.roll(jnp.where(low_half, parts[6 + digit], parts[3 + digit]), 64, 1)
                    for digit in range(3)
                ]
                product_hat[pl.ds(pl.multiple_of(place * 8, 8), 8), :] = folded(*totals)

    tables[0].wait()
    wait_plane(1, plane_recv)
    transform_blocks(1)
    wait_line(0, line_recv)
    transform_blocks(0)
    prepare_left()
    wait_plane(3, plane_recv)
    transform_blocks(3)
    wait_plane(4, plane_recv)
    transform_blocks(4)
    wait_line(2, line_recv)
    transform_blocks(2)
    multiply()

    parity = lax.rem(z_lo, 2)
    tables[1].wait()

    @pl.loop(0, LINE // 2, unroll=BLOCK_UNROLL)
    def _(pair):
        wide = jnp.concatenate(
            [product_hat[pl.ds(pair * 2 + side, LENGTH, stride=8), :] for side in range(2)], axis=1
        )
        values = folded(*thirds(matmul(back_ref[parity], stacked_digits(wide))))
        for side in range(2):
            group = pair * 2 + side
            mine = values[:, LANES * side : LANES * side + LANES]
            for half in range(2):
                part = CHUNKS + half
                first = PLANE * half
                plane_out[part, pl.ds(pl.multiple_of(group * 32, 32), 32), :] = mine[
                    first : first + 32
                ]
                for z_of in range(4):
                    line_out[part, pl.ds(32 + group * 4 + z_of, 8, stride=64), :] = mine[
                        first + 32 + 8 * z_of : first + 40 + 8 * z_of
                    ]

    def half_rows(other):
        return pl.ds(pl.multiple_of(other * PLANE + 32, 32), 32)

    def half_copy(part, other):
        return pltpu.make_async_remote_copy(
            src_ref=line_out.at[part, half_rows(other)],
            dst_ref=line_in.at[part, half_rows(me_line)],
            send_sem=line_send.at[part],
            recv_sem=line_recv.at[part],
            device_id=line_device(other),
            device_id_type=MESH,
        )

    def send_half_line(part):
        @pl.loop(0, LINE - 1, unroll=LINE - 1)
        def _(step):
            half_copy(part, lax.rem(me_line + far_first(step), LINE)).start()

        line_in[part, half_rows(me_line), :] = line_out[part, half_rows(me_line), :]

    def wait_half_line(part, semaphore):
        span = line_in.at[part, pl.ds(0, (LINE - 1) * 32)]
        pltpu.make_async_copy(span, span, semaphore.at[part]).wait()

    def send_core(part, core_other, make):
        def put(other):
            if make is not None:
                plane_out[part, plane_rows(other)] = make(other)

        @pl.loop(0, 31, unroll=CORE_UNROLL)
        def _(step):
            other = core_partner(step, core_other)
            put(other)
            plane_copy(part, other).start()

        last = core_partner(31, core_other)
        put(last)

        @pl.when(core != core_other)
        def _():
            plane_copy(part, last).start()

        @pl.when(core == core_other)
        def _():
            plane_in[part, plane_rows(me_plane)] = plane_out[part, plane_rows(me_plane)]

    def wait_core_sent(part, core_other):
        @pl.when(core != core_other)
        def _():
            span = plane_in.at[part, pl.ds(0, 32 * LINE)]
            pltpu.make_async_copy(span, span, plane_send.at[part]).wait()

        @pl.when(core == core_other)
        def _():
            span = plane_in.at[part, pl.ds(0, 31 * LINE)]
            pltpu.make_async_copy(span, span, plane_send.at[part]).wait()

    for half in range(2):
        send_half_line(CHUNKS + half)
        send_core(CHUNKS + half, 0, None)
    for half in range(2):
        part, last = CHUNKS + half, CHUNKS + 2 + half

        @pl.when(core == 0)
        def _():
            wait_plane(part, plane_recv)
            send_line(
                last, lambda other: plane_in[part, pl.ds(other, PLANE, stride=LINE), :]
            )

        wait_half_line(part, line_recv)
        send_core(last, 1, lambda other: line_in[part, pl.ds(other, LINE, stride=PLANE), :])

    def coefficients(half):
        part = CHUNKS + 2 + half

        @pl.when(core == 0)
        def _():
            wait_line(part, line_recv)

        @pl.when(core == 1)
        def _():
            wait_plane(part, plane_recv)
            for line in range(LINE):
                line_in[part, line_rows(line), :] = plane_in[
                    part, pl.ds(line, PLANE, stride=LINE), :
                ]

        total = None
        for side in range(2):
            values = line_in[part, pl.ds(side * BLOCK, BLOCK), :]
            sums = folded(*thirds(matmul(point_back_ref[side], stacked_digits(values))))
            total = sums if total is None else reduced(total + sums)
        total = jnp.where(total < 0.0, total + float(modulus), total)
        out_ref[:, half * BLOCK : half * BLOCK + BLOCK] = (total / float(modulus)).T

    tables[2].wait()
    coefficients(0)
    coefficients(1)

    for part in range(CHUNKS):
        wait_line(part, line_send)
        wait_plane(part, plane_send)
    for half in range(2):
        wait_half_line(CHUNKS + half, line_send)
        wait_core_sent(CHUNKS + half, 0)
        wait_core_sent(CHUNKS + 2 + half, 1)

    @pl.when(core == 0)
    def _():
        for half in range(2):
            wait_line(CHUNKS + 2 + half, line_send)


PLANE_UNROLL = 7
CORE_UNROLL = 31
POINT_UNROLL = 2
BLOCK_UNROLL = 2
LEFT_UNROLL = 2
PRODUCT_UNROLL = 4


def shards(left_factor, right_factor):
    local, rows, depth = left_factor.shape
    left = left_factor.transpose(1, 2, 0).reshape(LANES, local)
    right = right_factor.transpose(1, 2, 0).reshape((CHUNKS - 1) * LANES, local)
    parts = CHUNKS + 4
    whole = pl.BlockSpec(memory_space=pltpu.VMEM)
    remote = pl.BlockSpec(memory_space=pl.ANY)
    buffer = pltpu.VMEM((parts, POINTS, LANES), jnp.float32)
    semaphores = pltpu.SemaphoreType.DMA((parts,))
    point, block = point_table(), block_table()
    back, point_back = block_back_table(), point_back_table()
    coeffs = pl.pallas_call(
        kernel,
        out_shape=jax.ShapeDtypeStruct((LANES, POINTS), jnp.float32),
        in_specs=[whole] * 3 + [remote] * 4,
        out_specs=whole,
        scratch_shapes=[
            pltpu.VMEM(table.shape, jnp.bfloat16) for table in (point, block, back, point_back)
        ]
        + [buffer] * 4
        + [
            pltpu.VMEM((LENGTH * 8, LANES), jnp.float32),
            pltpu.VMEM((LENGTH * 96, LANES), jnp.bfloat16),
            pltpu.VMEM((LENGTH * 32, LANES), jnp.float32),
            pltpu.VMEM((LENGTH * 8, LANES), jnp.float32),
        ]
        + [pltpu.SemaphoreType.DMA((LINE,)), pltpu.SemaphoreType.DMA((3,))]
        + [semaphores] * 4,
        compiler_params=pltpu.CompilerParams(
            collective_id=0, has_side_effects=True, vmem_limit_bytes=56 * 2**20
        ),
    )(
        left,
        right,
        jnp.asarray(row_order()),
        jnp.asarray(point),
        jnp.asarray(block),
        jnp.asarray(back),
        jnp.asarray(point_back),
    )
    return coeffs.reshape(rows, CD, 2 * local).transpose(2, 0, 1)


def solution(mesh):
    placed = P("deg", "row", None)
    return jax.shard_map(
        shards, mesh=mesh, in_specs=(placed, placed), out_specs=placed, check_vma=False
    )
```

```python
import numpy as np
import jax
import jax.numpy as jnp
from jax import lax
from jax.experimental import pallas as pl
from jax.experimental.pallas import tpu as pltpu
from jax.sharding import PartitionSpec as P

modulus = 7340033
generator = 3
inverse_modulus = 1.0 / modulus
modulus_high = float(modulus - 1)

BLOCK = 256
POINTS = 2 * BLOCK
KD = 64
CD = 64


def powers(root, exponents, order):
    table = np.ones(order, np.int64)
    for position in range(1, order):
        table[position] = table[position - 1] * root % modulus
    return table[exponents % order]


def digit_rows(values):
    centred = np.where(values > modulus // 2, values - modulus, values)
    digits = []
    for _ in range(2):
        low = (centred + 128) % 256 - 128
        digits.append(low)
        centred = (centred - low) // 256
    digits.append(centred)
    return np.concatenate(digits, axis=0).astype(jnp.bfloat16)


MESH = pl.DeviceIdType.MESH
LANES = 128
BLOCKS = 64
LENGTH = 2 * BLOCKS
CHUNKS = 5
LINE = 8
PLANE = 64


def stacked_columns(values):
    return np.concatenate([values * 256**digit % modulus for digit in range(3)], axis=1)


def block_order():
    return np.arange(BLOCKS).reshape(8, 4, 2).transpose(2, 1, 0).reshape(BLOCKS)


def point_table():
    root = pow(generator, (modulus - 1) // POINTS, modulus)
    exponents = np.arange(POINTS)[:, None] * np.arange(BLOCK)[None, :]
    rows = digit_rows(stacked_columns(powers(root, exponents, POINTS)))
    rows = rows.reshape(3, LINE, PLANE, 3 * BLOCK).transpose(1, 0, 2, 3)
    return rows.reshape(LINE, 3 * PLANE, 3 * BLOCK)


def block_table():
    root = pow(generator, (modulus - 1) // LENGTH, modulus)
    exponents = np.arange(LENGTH)[:, None] * block_order()[None, :]
    return digit_rows(stacked_columns(powers(root, exponents, LENGTH)))


def block_back_table():
    root = pow(generator, (modulus - 1) // LENGTH, modulus)
    signed = []
    for sign in (1, -1):
        carry = 1 + sign * powers(root, np.arange(LENGTH), LENGTH)
        for half in range(2):
            rows = 2 * block_order() + half
            table = powers(root, -rows[:, None] * np.arange(LENGTH)[None, :], LENGTH)
            signed.append(digit_rows(stacked_columns(table * carry[None, :] % modulus)))
    return np.stack(signed)


def point_back_table():
    root = pow(generator, (modulus - 1) // POINTS, modulus)
    exponents = -np.arange(BLOCK)[:, None] * np.arange(POINTS)[None, :]
    scale = pow(2 * BLOCKS * POINTS, modulus - 2, modulus)
    table = powers(root, exponents, POINTS) * scale % modulus
    return np.stack(
        [digit_rows(stacked_columns(table[:, part : part + BLOCK])) for part in (0, BLOCK)]
    )


def row_order():
    source = np.arange(LANES).reshape(2, 8, 4, 2).transpose(0, 3, 1, 2).reshape(LANES)
    matrix = np.zeros((LANES, LANES), np.float32)
    matrix[np.arange(LANES), source] = 1.0
    return matrix.astype(jnp.bfloat16)


def reduced(values):
    quotient = jnp.round(values * inverse_modulus)
    return (values - quotient * modulus_high) - quotient


def folded(low, middle, high):
    return reduced(reduced((reduced(high * 256.0) + middle) * 256.0) + low)


def digits_of(values):
    high = jnp.round(values * (1.0 / 65536.0))
    rest = values - high * 65536.0
    middle = jnp.round(rest * (1.0 / 256.0))
    return [rest - middle * 256.0, middle, high]


def stacked_digits(values, axis=0):
    return jnp.concatenate([digit.astype(jnp.bfloat16) for digit in digits_of(values)], axis=axis)


def matmul(left, right):
    return jnp.dot(left, right, preferred_element_type=jnp.float32)


def matmul_transposed(left, right):
    return lax.dot_general(
        left, right, (((1,), (1,)), ((), ())), preferred_element_type=jnp.float32
    )


def thirds(sums):
    rows = sums.shape[0] // 3
    return [sums[part * rows : (part + 1) * rows] for part in range(3)]


def kernel(
    left_ref,
    right_ref,
    order_ref,
    point_hbm,
    block_hbm,
    back_hbm,
    point_back_hbm,
    out_ref,
    point_ref,
    block_ref,
    back_ref,
    point_back_ref,
    line_out,
    line_in,
    plane_out,
    plane_in,
    left_hat,
    left_digits,
    right_hat,
    product_hat,
    point_sem,
    table_sem,
    line_send,
    line_recv,
    plane_send,
    plane_recv,
):
    deg = lax.axis_index("deg")
    row = lax.axis_index("row")
    rest = lax.rem(deg, 8)
    me_line = deg // 8
    core = lax.rem(rest, 2)
    z_lo = rest // 2
    me_plane = core * 32 + row * 4 + z_lo

    def point_copy(other):
        return pltpu.make_async_copy(point_hbm.at[other], point_ref.at[other], point_sem.at[other])

    for other in range(LINE):
        point_copy(other).start()

    def line_device(other):
        return (other * 8 + rest, row)

    def plane_device(other):
        device = me_line * 8 + lax.rem(other, 4) * 2 + other // 32
        return (device, lax.rem(other // 4, 8))

    barrier = pltpu.get_barrier_semaphore()

    @pl.loop(1, LINE, unroll=LINE - 1)
    def _(step):
        pl.semaphore_signal(
            barrier,
            inc=1,
            device_id=line_device(lax.rem(me_line + step, LINE)),
            device_id_type=MESH,
        )

    @pl.loop(1, PLANE, unroll=PLANE_UNROLL)
    def _(step):
        pl.semaphore_signal(
            barrier,
            inc=1,
            device_id=plane_device(lax.rem(me_plane + step, PLANE)),
            device_id_type=MESH,
        )

    tables = [
        pltpu.make_async_copy(source, target, table_sem.at[index])
        for index, (source, target) in enumerate(
            [(block_hbm, block_ref), (back_hbm, back_ref), (point_back_hbm, point_back_ref)]
        )
    ]
    for table in tables:
        table.start()

    def line_rows(other):
        return pl.ds(pl.multiple_of(other * PLANE, PLANE), PLANE)

    def plane_rows(other):
        return pl.ds(pl.multiple_of(other * LINE, LINE), LINE)

    def line_copy(part, other):
        return pltpu.make_async_remote_copy(
            src_ref=line_out.at[part, line_rows(other)],
            dst_ref=line_in.at[part, line_rows(me_line)],
            send_sem=line_send.at[part],
            recv_sem=line_recv.at[part],
            device_id=line_device(other),
            device_id_type=MESH,
        )

    def plane_copy(part, other):
        return pltpu.make_async_remote_copy(
            src_ref=plane_out.at[part, plane_rows(other)],
            dst_ref=plane_in.at[part, plane_rows(me_plane)],
            send_sem=plane_send.at[part],
            recv_sem=plane_recv.at[part],
            device_id=plane_device(other),
            device_id_type=MESH,
        )

    def wait_line(part, semaphore):
        span = line_in.at[part, pl.ds(0, (LINE - 1) * PLANE)]
        pltpu.make_async_copy(span, span, semaphore.at[part]).wait()

    def wait_plane(part, semaphore):
        span = plane_in.at[part, pl.ds(0, (PLANE - 1) * LINE)]
        pltpu.make_async_copy(span, span, semaphore.at[part]).wait()

    def far_first(step):
        half = step // 2
        odd = lax.rem(step, 2)
        return odd * (3 - half) + (1 - odd) * (4 + half)

    def core_partner(step, core_other):
        pair = step // 8
        odd = lax.rem(pair, 2)
        shift = odd * (1 - pair // 2) + (1 - odd) * (2 + pair // 2)
        x_other = lax.rem(row // 2 + shift, 4)
        z_here = lax.rem(row, 2) * 4 + z_lo
        z_other = lax.rem(z_here + far_first(lax.rem(step, 8)), 8)
        return core_other * 32 + (x_other * 2 + z_other // 4) * 4 + lax.rem(z_other, 4)

    def plane_partner(step):
        outer = step // 8
        core_other = lax.rem(core + 1 - lax.rem(outer, 2), 2)
        return core_partner(outer // 2 * 8 + lax.rem(step, 8), core_other)

    def send_plane(part, make):
        @pl.loop(0, PLANE - 1, unroll=PLANE_UNROLL)
        def _(step):
            other = plane_partner(step)
            if make is not None:
                plane_out[part, plane_rows(other)] = make(other)
            plane_copy(part, other).start()

        own = plane_out[part, plane_rows(me_plane)] if make is None else make(me_plane)
        plane_in[part, plane_rows(me_plane)] = own

    def send_line(part, make):
        @pl.loop(0, LINE - 1, unroll=LINE - 1)
        def _(step):
            other = lax.rem(me_line + far_first(step), LINE)
            if make is not None:
                line_out[part, line_rows(other)] = make(other)
            line_copy(part, other).start()

        own = line_out[part, line_rows(me_line)] if make is None else make(me_line)
        line_in[part, line_rows(me_line)] = own

    def line_to_plane(part):
        send_plane(part, lambda other: line_in[part, pl.ds(other, LINE, stride=PLANE), :])

    def plane_to_line(part):
        send_line(part, lambda other: plane_in[part, pl.ds(other, PLANE, stride=LINE), :])

    def right_digits(first, count):
        return stacked_digits(right_ref[pl.ds((first - 1) * LANES, count * LANES), :], axis=1)

    def points_of(other, stacked):
        return folded(*thirds(matmul_transposed(point_ref[other], stacked)))

    left = stacked_digits(left_ref[...], axis=1)
    left = matmul(order_ref[...], left).astype(jnp.bfloat16)
    stacked = jnp.concatenate([left, right_digits(1, 1)], axis=0)

    @pl.loop(0, LINE, unroll=POINT_UNROLL)
    def _(other):
        point_copy(other).wait()
        values = points_of(other, stacked)
        plane_out[0, pl.ds(other, PLANE, stride=LINE), :] = values[:, :LANES]
        line_out[1, line_rows(other), :] = values[:, LANES:]

    pl.semaphore_wait(barrier, LINE + PLANE - 2)
    send_line(1, None)
    send_plane(0, None)

    stacked_more = right_digits(2, 2)

    @pl.loop(0, LINE, unroll=POINT_UNROLL)
    def _(other):
        values = points_of(other, stacked_more)
        plane_out[2, pl.ds(other, PLANE, stride=LINE), :] = values[:, :LANES]
        line_out[3, line_rows(other), :] = values[:, LANES:]

    send_line(3, None)
    send_plane(2, None)

    stacked_last = right_digits(4, 1)

    @pl.loop(0, LINE, unroll=POINT_UNROLL)
    def _(other):
        line_out[4, line_rows(other), :] = points_of(other, stacked_last)

    send_line(4, None)
    wait_line(1, line_recv)
    line_to_plane(1)
    wait_plane(0, plane_recv)
    plane_to_line(0)
    wait_line(3, line_recv)
    line_to_plane(3)
    wait_plane(2, plane_recv)
    plane_to_line(2)
    wait_line(4, line_recv)
    line_to_plane(4)

    def blocks_of(part, group):
        if part in (0, 2):
            return jnp.concatenate(
                [
                    line_in[part, pl.ds(group * 4 + index // 4 * 32 + index % 4, 8, stride=64), :]
                    for index in range(LINE)
                ],
                axis=0,
            )
        return jnp.concatenate(
            [
                plane_in[part, pl.ds(pl.multiple_of(side * 256 + group * 32, 32), 32), :]
                for side in range(2)
            ],
            axis=0,
        )

    def transform_blocks(part):
        @pl.loop(0, LINE // 2, unroll=BLOCK_UNROLL)
        def _(pair):
            wide = jnp.concatenate(
                [blocks_of(part, pair * 2), blocks_of(part, pair * 2 + 1)], axis=1
            )
            spectrum = folded(*thirds(matmul(block_ref[...], stacked_digits(wide))))
            for side in range(2):
                group = pair * 2 + side
                values = spectrum[:, LANES * side : LANES * side + LANES]
                if part == 0:
                    left_hat[pl.ds(group, LENGTH, stride=8), :] = values
                else:
                    right_hat[pl.ds(group * 4 + part - 1, LENGTH, stride=32), :] = values

    batch = 8
    lane = lax.broadcasted_iota(jnp.int32, (8 * batch, LANES), 1)
    window = lane // 32
    low_half = lax.broadcasted_iota(jnp.int32, (8, LANES), 1) < 64

    def prepare_left():
        @pl.loop(0, LENGTH // batch, unroll=LEFT_UNROLL)
        def _(step):
            base = pl.multiple_of(step * 8 * batch, 8 * batch)
            left = left_hat[pl.ds(base, 8 * batch), :]
            factors = []
            for choice in range(4):
                spread = jnp.where(window == choice, left, 0.0)
                for shift in (64, 32):
                    spread = spread + pltpu.roll(spread, shift, 1)
                once = reduced(spread * 256.0)
                twice = reduced(once * 256.0)
                spread = jnp.where(window == 0, spread, jnp.where(window == 1, once, twice))
                factors.append(digits_of(jnp.where(window < 3, spread, 0.0)))
            for index in range(batch):
                rows = slice(8 * index, 8 * index + 8)
                start = pl.multiple_of((step * batch + index) * 96, 96)
                left_digits[pl.ds(start, 96), :] = jnp.concatenate(
                    [digit[rows] for factor in factors for digit in factor], axis=0
                ).astype(jnp.bfloat16)

    def multiply():
        @pl.loop(0, LENGTH // batch, unroll=PRODUCT_UNROLL)
        def _(step):
            for index in range(batch):
                place = step * batch + index
                left = left_digits[pl.ds(pl.multiple_of(place * 96, 96), 96), :]
                right = digits_of(right_hat[pl.ds(pl.multiple_of(place * 32, 32), 32), :])
                right = jnp.concatenate(right + [right[2]], axis=0).astype(jnp.bfloat16)
                sums = matmul(left, right)
                parts = [sums[8 * part : 8 * part + 8] for part in range(12)]
                totals = [
                    jnp.where(low_half, parts[digit], parts[9 + digit])
                    + pltpu.roll(jnp.where(low_half, parts[6 + digit], parts[3 + digit]), 64, 1)
                    for digit in range(3)
                ]
                product_hat[pl.ds(pl.multiple_of(place * 8, 8), 8), :] = folded(*totals)

    tables[0].wait()
    wait_plane(1, plane_recv)
    transform_blocks(1)
    wait_line(0, line_recv)
    transform_blocks(0)
    prepare_left()
    wait_plane(3, plane_recv)
    transform_blocks(3)
    wait_plane(4, plane_recv)
    transform_blocks(4)
    wait_line(2, line_recv)
    transform_blocks(2)
    multiply()

    parity = lax.rem(z_lo, 2)
    tables[1].wait()

    def leave_blocks(half):
        part = CHUNKS + half

        @pl.loop(0, LINE // 2, unroll=BLOCK_UNROLL)
        def _(pair):
            wide = jnp.concatenate(
                [product_hat[pl.ds(pair * 2 + side, LENGTH, stride=8), :] for side in range(2)],
                axis=1,
            )
            values = folded(*thirds(matmul(back_ref[parity * 2 + half], stacked_digits(wide))))
            for side in range(2):
                group = pair * 2 + side
                mine = values[:, LANES * side : LANES * side + LANES]
                plane_out[part, pl.ds(pl.multiple_of(group * 32, 32), 32), :] = mine[:32]
                for z_of in range(4):
                    line_out[part, pl.ds(32 + group * 4 + z_of, 8, stride=64), :] = mine[
                        32 + 8 * z_of : 40 + 8 * z_of
                    ]

    def half_rows(other):
        return pl.ds(pl.multiple_of(other * PLANE + 32, 32), 32)

    def half_copy(part, other):
        return pltpu.make_async_remote_copy(
            src_ref=line_out.at[part, half_rows(other)],
            dst_ref=line_in.at[part, half_rows(me_line)],
            send_sem=line_send.at[part],
            recv_sem=line_recv.at[part],
            device_id=line_device(other),
            device_id_type=MESH,
        )

    def send_half_line(part):
        @pl.loop(0, LINE - 1, unroll=LINE - 1)
        def _(step):
            half_copy(part, lax.rem(me_line + far_first(step), LINE)).start()

        line_in[part, half_rows(me_line), :] = line_out[part, half_rows(me_line), :]

    def wait_half_line(part, semaphore):
        span = line_in.at[part, pl.ds(0, (LINE - 1) * 32)]
        pltpu.make_async_copy(span, span, semaphore.at[part]).wait()

    def send_core(part, core_other, make):
        def put(other):
            if make is not None:
                plane_out[part, plane_rows(other)] = make(other)

        @pl.loop(0, 31, unroll=CORE_UNROLL)
        def _(step):
            other = core_partner(step, core_other)
            put(other)
            plane_copy(part, other).start()

        last = core_partner(31, core_other)
        put(last)

        @pl.when(core != core_other)
        def _():
            plane_copy(part, last).start()

        @pl.when(core == core_other)
        def _():
            plane_in[part, plane_rows(me_plane)] = plane_out[part, plane_rows(me_plane)]

    def wait_core_sent(part, core_other):
        @pl.when(core != core_other)
        def _():
            span = plane_in.at[part, pl.ds(0, 32 * LINE)]
            pltpu.make_async_copy(span, span, plane_send.at[part]).wait()

        @pl.when(core == core_other)
        def _():
            span = plane_in.at[part, pl.ds(0, 31 * LINE)]
            pltpu.make_async_copy(span, span, plane_send.at[part]).wait()

    for half in range(2):
        leave_blocks(half)
        send_half_line(CHUNKS + half)
        send_core(CHUNKS + half, 0, None)
    for half in range(2):
        part, last = CHUNKS + half, CHUNKS + 2 + half

        @pl.when(core == 0)
        def _():
            wait_plane(part, plane_recv)
            send_line(
                last, lambda other: plane_in[part, pl.ds(other, PLANE, stride=LINE), :]
            )

        wait_half_line(part, line_recv)
        send_core(last, 1, lambda other: line_in[part, pl.ds(other, LINE, stride=PLANE), :])

    def coefficients(half):
        part = CHUNKS + 2 + half

        @pl.when(core == 0)
        def _():
            wait_line(part, line_recv)

        @pl.when(core == 1)
        def _():
            wait_plane(part, plane_recv)
            for line in range(LINE):
                line_in[part, line_rows(line), :] = plane_in[
                    part, pl.ds(line, PLANE, stride=LINE), :
                ]

        total = None
        for side in range(2):
            values = line_in[part, pl.ds(side * BLOCK, BLOCK), :]
            sums = folded(*thirds(matmul(point_back_ref[side], stacked_digits(values))))
            total = sums if total is None else reduced(total + sums)
        total = jnp.where(total < 0.0, total + float(modulus), total)
        out_ref[:, half * BLOCK : half * BLOCK + BLOCK] = (total / float(modulus)).T

    tables[2].wait()
    coefficients(0)
    coefficients(1)

    for part in range(CHUNKS):
        wait_line(part, line_send)
        wait_plane(part, plane_send)
    for half in range(2):
        wait_half_line(CHUNKS + half, line_send)
        wait_core_sent(CHUNKS + half, 0)
        wait_core_sent(CHUNKS + 2 + half, 1)

    @pl.when(core == 0)
    def _():
        for half in range(2):
            wait_line(CHUNKS + 2 + half, line_send)


PLANE_UNROLL = 7
CORE_UNROLL = 31
POINT_UNROLL = 4
BLOCK_UNROLL = 4
LEFT_UNROLL = 2
PRODUCT_UNROLL = 8


def shards(left_factor, right_factor):
    local, rows, depth = left_factor.shape
    left = left_factor.transpose(1, 2, 0).reshape(LANES, local)
    right = right_factor.transpose(1, 2, 0).reshape((CHUNKS - 1) * LANES, local)
    parts = CHUNKS + 4
    whole = pl.BlockSpec(memory_space=pltpu.VMEM)
    remote = pl.BlockSpec(memory_space=pl.ANY)
    buffer = pltpu.VMEM((parts, POINTS, LANES), jnp.float32)
    semaphores = pltpu.SemaphoreType.DMA((parts,))
    point, block = point_table(), block_table()
    back, point_back = block_back_table(), point_back_table()
    coeffs = pl.pallas_call(
        kernel,
        out_shape=pltpu.VMEM((LANES, POINTS), jnp.float32),
        in_specs=[whole] * 3 + [remote] * 4,
        out_specs=whole,
        scratch_shapes=[
            pltpu.VMEM(table.shape, jnp.bfloat16) for table in (point, block, back, point_back)
        ]
        + [buffer] * 4
        + [
            pltpu.VMEM((LENGTH * 8, LANES), jnp.float32),
            pltpu.VMEM((LENGTH * 96, LANES), jnp.bfloat16),
            pltpu.VMEM((LENGTH * 32, LANES), jnp.float32),
            pltpu.VMEM((LENGTH * 8, LANES), jnp.float32),
        ]
        + [pltpu.SemaphoreType.DMA((LINE,)), pltpu.SemaphoreType.DMA((3,))]
        + [semaphores] * 4,
        compiler_params=pltpu.CompilerParams(
            collective_id=0, has_side_effects=True, vmem_limit_bytes=56 * 2**20
        ),
    )(
        left,
        right,
        jnp.asarray(row_order()),
        jnp.asarray(point),
        jnp.asarray(block),
        jnp.asarray(back),
        jnp.asarray(point_back),
    )
    return coeffs.reshape(rows, CD, 2 * local).transpose(2, 0, 1)


def solution(mesh):
    placed = P("deg", "row", None)
    return jax.shard_map(
        shards, mesh=mesh, in_specs=(placed, placed), out_specs=placed, check_vma=False
    )
```

```python
import numpy as np
import jax
import jax.numpy as jnp
from jax import lax
from jax.experimental import pallas as pl
from jax.experimental.pallas import tpu as pltpu
from jax.sharding import PartitionSpec as P

modulus = 7340033
generator = 3
inverse_modulus = 1.0 / modulus
modulus_high = float(modulus - 1)

BLOCK = 256
POINTS = 2 * BLOCK
KD = 64
CD = 64


def powers(root, exponents, order):
    table = np.ones(order, np.int64)
    for position in range(1, order):
        table[position] = table[position - 1] * root % modulus
    return table[exponents % order]


def digit_rows(values):
    centred = np.where(values > modulus // 2, values - modulus, values)
    digits = []
    for _ in range(2):
        low = (centred + 128) % 256 - 128
        digits.append(low)
        centred = (centred - low) // 256
    digits.append(centred)
    return np.concatenate(digits, axis=0).astype(jnp.bfloat16)


MESH = pl.DeviceIdType.MESH
LANES = 128
BLOCKS = 64
LENGTH = 2 * BLOCKS
CHUNKS = 5
LINE = 8
PLANE = 64


def stacked_columns(values):
    return np.concatenate([values * 256**digit % modulus for digit in range(3)], axis=1)


def block_order():
    return np.arange(BLOCKS).reshape(8, 4, 2).transpose(2, 1, 0).reshape(BLOCKS)


def point_table():
    root = pow(generator, (modulus - 1) // POINTS, modulus)
    exponents = np.arange(POINTS)[:, None] * np.arange(BLOCK)[None, :]
    rows = digit_rows(stacked_columns(powers(root, exponents, POINTS)))
    rows = rows.reshape(3, LINE, PLANE, 3 * BLOCK).transpose(1, 0, 2, 3)
    return rows.reshape(LINE, 3 * PLANE, 3 * BLOCK)


def block_table():
    root = pow(generator, (modulus - 1) // LENGTH, modulus)
    exponents = np.arange(LENGTH)[:, None] * block_order()[None, :]
    return digit_rows(stacked_columns(powers(root, exponents, LENGTH)))


def block_back_table():
    root = pow(generator, (modulus - 1) // LENGTH, modulus)
    signed = []
    for sign in (1, -1):
        carry = 1 + sign * powers(root, np.arange(LENGTH), LENGTH)
        for half in range(2):
            rows = 2 * block_order() + half
            table = powers(root, -rows[:, None] * np.arange(LENGTH)[None, :], LENGTH)
            signed.append(digit_rows(stacked_columns(table * carry[None, :] % modulus)))
    return np.stack(signed)


def point_back_table():
    root = pow(generator, (modulus - 1) // POINTS, modulus)
    exponents = -np.arange(BLOCK)[:, None] * np.arange(POINTS)[None, :]
    scale = pow(2 * BLOCKS * POINTS, modulus - 2, modulus)
    table = powers(root, exponents, POINTS) * scale % modulus
    return np.stack(
        [digit_rows(stacked_columns(table[:, part : part + BLOCK])) for part in (0, BLOCK)]
    )


def row_order():
    source = np.arange(LANES).reshape(2, 8, 4, 2).transpose(0, 3, 1, 2).reshape(LANES)
    matrix = np.zeros((LANES, LANES), np.float32)
    matrix[np.arange(LANES), source] = 1.0
    return matrix.astype(jnp.bfloat16)


def reduced(values):
    quotient = jnp.round(values * inverse_modulus)
    return (values - quotient * modulus_high) - quotient


def folded(low, middle, high):
    return reduced(reduced((reduced(high * 256.0) + middle) * 256.0) + low)


def digits_of(values):
    high = jnp.round(values * (1.0 / 65536.0))
    rest = values - high * 65536.0
    middle = jnp.round(rest * (1.0 / 256.0))
    return [rest - middle * 256.0, middle, high]


def stacked_digits(values, axis=0):
    return jnp.concatenate([digit.astype(jnp.bfloat16) for digit in digits_of(values)], axis=axis)


def matmul(left, right):
    return jnp.dot(left, right, preferred_element_type=jnp.float32)


def matmul_transposed(left, right):
    return lax.dot_general(
        left, right, (((1,), (1,)), ((), ())), preferred_element_type=jnp.float32
    )


def thirds(sums):
    rows = sums.shape[0] // 3
    return [sums[part * rows : (part + 1) * rows] for part in range(3)]


def kernel(
    left_ref,
    right_ref,
    order_ref,
    point_hbm,
    block_hbm,
    back_hbm,
    point_back_hbm,
    out_ref,
    point_ref,
    block_ref,
    back_ref,
    point_back_ref,
    line_out,
    line_in,
    plane_out,
    plane_in,
    left_hat,
    left_digits,
    right_hat,
    product_hat,
    point_sem,
    table_sem,
    line_send,
    line_recv,
    plane_send,
    plane_recv,
):
    deg = lax.axis_index("deg")
    row = lax.axis_index("row")
    rest = lax.rem(deg, 8)
    me_line = deg // 8
    core = lax.rem(rest, 2)
    z_lo = rest // 2
    me_plane = core * 32 + row * 4 + z_lo

    def point_copy(other):
        return pltpu.make_async_copy(point_hbm.at[other], point_ref.at[other], point_sem.at[other])

    for other in range(LINE):
        point_copy(other).start()

    def line_device(other):
        return (other * 8 + rest, row)

    def plane_device(other):
        device = me_line * 8 + lax.rem(other, 4) * 2 + other // 32
        return (device, lax.rem(other // 4, 8))

    barrier = pltpu.get_barrier_semaphore()

    @pl.loop(1, LINE, unroll=LINE - 1)
    def _(step):
        pl.semaphore_signal(
            barrier,
            inc=1,
            device_id=line_device(lax.rem(me_line + step, LINE)),
            device_id_type=MESH,
        )

    @pl.loop(1, PLANE, unroll=PLANE_UNROLL)
    def _(step):
        pl.semaphore_signal(
            barrier,
            inc=1,
            device_id=plane_device(lax.rem(me_plane + step, PLANE)),
            device_id_type=MESH,
        )

    tables = [
        pltpu.make_async_copy(source, target, table_sem.at[index])
        for index, (source, target) in enumerate(
            [(block_hbm, block_ref), (back_hbm, back_ref), (point_back_hbm, point_back_ref)]
        )
    ]
    for table in tables:
        table.start()

    def line_rows(other):
        return pl.ds(pl.multiple_of(other * PLANE, PLANE), PLANE)

    def plane_rows(other):
        return pl.ds(pl.multiple_of(other * LINE, LINE), LINE)

    def line_copy(part, other):
        return pltpu.make_async_remote_copy(
            src_ref=line_out.at[part, line_rows(other)],
            dst_ref=line_in.at[part, line_rows(me_line)],
            send_sem=line_send.at[part],
            recv_sem=line_recv.at[part],
            device_id=line_device(other),
            device_id_type=MESH,
        )

    def plane_copy(part, other):
        return pltpu.make_async_remote_copy(
            src_ref=plane_out.at[part, plane_rows(other)],
            dst_ref=plane_in.at[part, plane_rows(me_plane)],
            send_sem=plane_send.at[part],
            recv_sem=plane_recv.at[part],
            device_id=plane_device(other),
            device_id_type=MESH,
        )

    def wait_line(part, semaphore):
        span = line_in.at[part, pl.ds(0, (LINE - 1) * PLANE)]
        pltpu.make_async_copy(span, span, semaphore.at[part]).wait()

    def wait_plane(part, semaphore):
        span = plane_in.at[part, pl.ds(0, (PLANE - 1) * LINE)]
        pltpu.make_async_copy(span, span, semaphore.at[part]).wait()

    def far_first(step):
        half = step // 2
        odd = lax.rem(step, 2)
        return odd * (3 - half) + (1 - odd) * (4 + half)

    def core_partner(step, core_other):
        pair = step // 8
        odd = lax.rem(pair, 2)
        shift = odd * (1 - pair // 2) + (1 - odd) * (2 + pair // 2)
        x_other = lax.rem(row // 2 + shift, 4)
        z_here = lax.rem(row, 2) * 4 + z_lo
        z_other = lax.rem(z_here + far_first(lax.rem(step, 8)), 8)
        return core_other * 32 + (x_other * 2 + z_other // 4) * 4 + lax.rem(z_other, 4)

    def plane_partner(step):
        outer = step // 8
        core_other = lax.rem(core + 1 - lax.rem(outer, 2), 2)
        return core_partner(outer // 2 * 8 + lax.rem(step, 8), core_other)

    def send_plane(part, make):
        @pl.loop(0, PLANE - 1, unroll=PLANE_UNROLL)
        def _(step):
            other = plane_partner(step)
            if make is not None:
                plane_out[part, plane_rows(other)] = make(other)
            plane_copy(part, other).start()

        own = plane_out[part, plane_rows(me_plane)] if make is None else make(me_plane)
        plane_in[part, plane_rows(me_plane)] = own

    def send_line(part, make):
        @pl.loop(0, LINE - 1, unroll=LINE - 1)
        def _(step):
            other = lax.rem(me_line + far_first(step), LINE)
            if make is not None:
                line_out[part, line_rows(other)] = make(other)
            line_copy(part, other).start()

        own = line_out[part, line_rows(me_line)] if make is None else make(me_line)
        line_in[part, line_rows(me_line)] = own

    def line_to_plane(part):
        send_plane(part, lambda other: line_in[part, pl.ds(other, LINE, stride=PLANE), :])

    def plane_to_line(part):
        send_line(part, lambda other: plane_in[part, pl.ds(other, PLANE, stride=LINE), :])

    def right_digits(first, count):
        return stacked_digits(right_ref[pl.ds((first - 1) * LANES, count * LANES), :], axis=1)

    def points_of(other, stacked):
        return folded(*thirds(matmul_transposed(point_ref[other], stacked)))

    left = stacked_digits(left_ref[...], axis=1)
    left = matmul(order_ref[...], left).astype(jnp.bfloat16)
    stacked = jnp.concatenate([left, right_digits(1, 1)], axis=0)

    pl.semaphore_wait(barrier, LINE + PLANE - 2)

    @pl.loop(0, LINE, unroll=POINT_UNROLL)
    def _(step):
        other = lax.rem(me_line + 1 + step, LINE)
        point_copy(other).wait()
        values = points_of(other, stacked)
        plane_out[0, pl.ds(other, PLANE, stride=LINE), :] = values[:, :LANES]
        line_out[1, line_rows(other), :] = values[:, LANES:]

        @pl.when(step < LINE - 1)
        def _():
            line_copy(1, other).start()

    line_in[1, line_rows(me_line), :] = line_out[1, line_rows(me_line), :]
    send_plane(0, None)

    stacked_more = right_digits(2, 2)

    @pl.loop(0, LINE, unroll=POINT_UNROLL)
    def _(other):
        values = points_of(other, stacked_more)
        plane_out[2, pl.ds(other, PLANE, stride=LINE), :] = values[:, :LANES]
        line_out[3, line_rows(other), :] = values[:, LANES:]

    send_line(3, None)
    send_plane(2, None)

    stacked_last = right_digits(4, 1)

    @pl.loop(0, LINE, unroll=POINT_UNROLL)
    def _(other):
        line_out[4, line_rows(other), :] = points_of(other, stacked_last)

    send_line(4, None)
    wait_line(1, line_recv)
    line_to_plane(1)
    wait_plane(0, plane_recv)
    plane_to_line(0)
    wait_line(3, line_recv)
    line_to_plane(3)
    wait_plane(2, plane_recv)
    plane_to_line(2)
    wait_line(4, line_recv)
    line_to_plane(4)

    def blocks_of(part, group):
        if part in (0, 2):
            return jnp.concatenate(
                [
                    line_in[part, pl.ds(group * 4 + index // 4 * 32 + index % 4, 8, stride=64), :]
                    for index in range(LINE)
                ],
                axis=0,
            )
        return jnp.concatenate(
            [
                plane_in[part, pl.ds(pl.multiple_of(side * 256 + group * 32, 32), 32), :]
                for side in range(2)
            ],
            axis=0,
        )

    def transform_blocks(part):
        @pl.loop(0, LINE // 2, unroll=BLOCK_UNROLL)
        def _(pair):
            wide = jnp.concatenate(
                [blocks_of(part, pair * 2), blocks_of(part, pair * 2 + 1)], axis=1
            )
            spectrum = folded(*thirds(matmul(block_ref[...], stacked_digits(wide))))
            for side in range(2):
                group = pair * 2 + side
                values = spectrum[:, LANES * side : LANES * side + LANES]
                if part == 0:
                    left_hat[pl.ds(group, LENGTH, stride=8), :] = values
                else:
                    right_hat[pl.ds(group * 4 + part - 1, LENGTH, stride=32), :] = values

    batch = 8
    lane = lax.broadcasted_iota(jnp.int32, (8 * batch, LANES), 1)
    window = lane // 32
    low_half = lax.broadcasted_iota(jnp.int32, (8, LANES), 1) < 64

    def prepare_left():
        @pl.loop(0, LENGTH // batch, unroll=LEFT_UNROLL)
        def _(step):
            base = pl.multiple_of(step * 8 * batch, 8 * batch)
            left = left_hat[pl.ds(base, 8 * batch), :]
            factors = []
            for choice in range(4):
                spread = jnp.where(window == choice, left, 0.0)
                for shift in (64, 32):
                    spread = spread + pltpu.roll(spread, shift, 1)
                once = reduced(spread * 256.0)
                twice = reduced(once * 256.0)
                spread = jnp.where(window == 0, spread, jnp.where(window == 1, once, twice))
                factors.append(digits_of(jnp.where(window < 3, spread, 0.0)))
            for index in range(batch):
                rows = slice(8 * index, 8 * index + 8)
                start = pl.multiple_of((step * batch + index) * 96, 96)
                left_digits[pl.ds(start, 96), :] = jnp.concatenate(
                    [digit[rows] for factor in factors for digit in factor], axis=0
                ).astype(jnp.bfloat16)

    def multiply():
        @pl.loop(0, LENGTH // batch, unroll=PRODUCT_UNROLL)
        def _(step):
            for index in range(batch):
                place = step * batch + index
                left = left_digits[pl.ds(pl.multiple_of(place * 96, 96), 96), :]
                right = digits_of(right_hat[pl.ds(pl.multiple_of(place * 32, 32), 32), :])
                right = jnp.concatenate(right + [right[2]], axis=0).astype(jnp.bfloat16)
                sums = matmul(left, right)
                parts = [sums[8 * part : 8 * part + 8] for part in range(12)]
                totals = [
                    jnp.where(low_half, parts[digit], parts[9 + digit])
                    + pltpu.roll(jnp.where(low_half, parts[6 + digit], parts[3 + digit]), 64, 1)
                    for digit in range(3)
                ]
                product_hat[pl.ds(pl.multiple_of(place * 8, 8), 8), :] = folded(*totals)

    tables[0].wait()
    wait_plane(1, plane_recv)
    transform_blocks(1)
    wait_line(0, line_recv)
    transform_blocks(0)
    prepare_left()
    wait_plane(3, plane_recv)
    transform_blocks(3)
    wait_plane(4, plane_recv)
    transform_blocks(4)
    wait_line(2, line_recv)
    transform_blocks(2)
    multiply()

    parity = lax.rem(z_lo, 2)
    tables[1].wait()

    def leave_blocks(half):
        part = CHUNKS + half

        @pl.loop(0, LINE // 2, unroll=BLOCK_UNROLL)
        def _(pair):
            wide = jnp.concatenate(
                [product_hat[pl.ds(pair * 2 + side, LENGTH, stride=8), :] for side in range(2)],
                axis=1,
            )
            values = folded(*thirds(matmul(back_ref[parity * 2 + half], stacked_digits(wide))))
            for side in range(2):
                group = pair * 2 + side
                mine = values[:, LANES * side : LANES * side + LANES]
                plane_out[part, pl.ds(pl.multiple_of(group * 32, 32), 32), :] = mine[:32]
                for z_of in range(4):
                    line_out[part, pl.ds(32 + group * 4 + z_of, 8, stride=64), :] = mine[
                        32 + 8 * z_of : 40 + 8 * z_of
                    ]

    def half_rows(other):
        return pl.ds(pl.multiple_of(other * PLANE + 32, 32), 32)

    def half_copy(part, other):
        return pltpu.make_async_remote_copy(
            src_ref=line_out.at[part, half_rows(other)],
            dst_ref=line_in.at[part, half_rows(me_line)],
            send_sem=line_send.at[part],
            recv_sem=line_recv.at[part],
            device_id=line_device(other),
            device_id_type=MESH,
        )

    def send_half_line(part):
        @pl.loop(0, LINE - 1, unroll=LINE - 1)
        def _(step):
            half_copy(part, lax.rem(me_line + far_first(step), LINE)).start()

        line_in[part, half_rows(me_line), :] = line_out[part, half_rows(me_line), :]

    def wait_half_line(part, semaphore):
        span = line_in.at[part, pl.ds(0, (LINE - 1) * 32)]
        pltpu.make_async_copy(span, span, semaphore.at[part]).wait()

    def send_core(part, core_other, make):
        def put(other):
            if make is not None:
                plane_out[part, plane_rows(other)] = make(other)

        @pl.loop(0, 31, unroll=CORE_UNROLL)
        def _(step):
            other = core_partner(step, core_other)
            put(other)
            plane_copy(part, other).start()

        last = core_partner(31, core_other)
        put(last)

        @pl.when(core != core_other)
        def _():
            plane_copy(part, last).start()

        @pl.when(core == core_other)
        def _():
            plane_in[part, plane_rows(me_plane)] = plane_out[part, plane_rows(me_plane)]

    def wait_core_sent(part, core_other):
        @pl.when(core != core_other)
        def _():
            span = plane_in.at[part, pl.ds(0, 32 * LINE)]
            pltpu.make_async_copy(span, span, plane_send.at[part]).wait()

        @pl.when(core == core_other)
        def _():
            span = plane_in.at[part, pl.ds(0, 31 * LINE)]
            pltpu.make_async_copy(span, span, plane_send.at[part]).wait()

    for half in range(2):
        leave_blocks(half)
        send_half_line(CHUNKS + half)
        send_core(CHUNKS + half, 0, None)
    for half in range(2):
        part, last = CHUNKS + half, CHUNKS + 2 + half

        @pl.when(core == 0)
        def _():
            wait_plane(part, plane_recv)
            send_line(
                last, lambda other: plane_in[part, pl.ds(other, PLANE, stride=LINE), :]
            )

        wait_half_line(part, line_recv)
        send_core(last, 1, lambda other: line_in[part, pl.ds(other, LINE, stride=PLANE), :])

    def coefficients(half):
        part = CHUNKS + 2 + half

        @pl.when(core == 0)
        def _():
            wait_line(part, line_recv)

        @pl.when(core == 1)
        def _():
            wait_plane(part, plane_recv)
            for line in range(LINE):
                line_in[part, line_rows(line), :] = plane_in[
                    part, pl.ds(line, PLANE, stride=LINE), :
                ]

        total = None
        for side in range(2):
            values = line_in[part, pl.ds(side * BLOCK, BLOCK), :]
            sums = folded(*thirds(matmul(point_back_ref[side], stacked_digits(values))))
            total = sums if total is None else reduced(total + sums)
        total = jnp.where(total < 0.0, total + float(modulus), total)
        out_ref[:, half * BLOCK : half * BLOCK + BLOCK] = (total / float(modulus)).T

    tables[2].wait()
    coefficients(0)
    coefficients(1)

    for part in range(CHUNKS):
        wait_line(part, line_send)
        wait_plane(part, plane_send)
    for half in range(2):
        wait_half_line(CHUNKS + half, line_send)
        wait_core_sent(CHUNKS + half, 0)
        wait_core_sent(CHUNKS + 2 + half, 1)

    @pl.when(core == 0)
    def _():
        for half in range(2):
            wait_line(CHUNKS + 2 + half, line_send)


PLANE_UNROLL = 7
CORE_UNROLL = 31
POINT_UNROLL = 4
BLOCK_UNROLL = 4
LEFT_UNROLL = 2
PRODUCT_UNROLL = 8


def shards(left_factor, right_factor):
    local, rows, depth = left_factor.shape
    left = left_factor.transpose(1, 2, 0).reshape(LANES, local)
    right = right_factor.transpose(1, 2, 0).reshape((CHUNKS - 1) * LANES, local)
    parts = CHUNKS + 4
    whole = pl.BlockSpec(memory_space=pltpu.VMEM)
    remote = pl.BlockSpec(memory_space=pl.ANY)
    buffer = pltpu.VMEM((parts, POINTS, LANES), jnp.float32)
    semaphores = pltpu.SemaphoreType.DMA((parts,))
    point, block = point_table(), block_table()
    back, point_back = block_back_table(), point_back_table()
    coeffs = pl.pallas_call(
        kernel,
        out_shape=pltpu.VMEM((LANES, POINTS), jnp.float32),
        in_specs=[whole] * 3 + [remote] * 4,
        out_specs=whole,
        scratch_shapes=[
            pltpu.VMEM(table.shape, jnp.bfloat16) for table in (point, block, back, point_back)
        ]
        + [buffer] * 4
        + [
            pltpu.VMEM((LENGTH * 8, LANES), jnp.float32),
            pltpu.VMEM((LENGTH * 96, LANES), jnp.bfloat16),
            pltpu.VMEM((LENGTH * 32, LANES), jnp.float32),
            pltpu.VMEM((LENGTH * 8, LANES), jnp.float32),
        ]
        + [pltpu.SemaphoreType.DMA((LINE,)), pltpu.SemaphoreType.DMA((3,))]
        + [semaphores] * 4,
        compiler_params=pltpu.CompilerParams(
            collective_id=0, has_side_effects=True, vmem_limit_bytes=56 * 2**20
        ),
    )(
        left,
        right,
        jnp.asarray(row_order()),
        jnp.asarray(point),
        jnp.asarray(block),
        jnp.asarray(back),
        jnp.asarray(point_back),
    )
    return coeffs.reshape(rows, CD, 2 * local).transpose(2, 0, 1)


def solution(mesh):
    placed = P("deg", "row", None)
    return jax.shard_map(
        shards, mesh=mesh, in_specs=(placed, placed), out_specs=placed, check_vma=False
    )
```
